256 devices in a mesh: group: 16 (over z, core), local: 16 (over y, x).
Axes of the slice: x: 4, y: 4, z: 8, core: 2. Of those that a mesh axis runs over, the one named last changes fastest.
Arguments:
- tokens: bfloat16 [16384, 4096], P(('group', 'local')), may hold values from -6 to 6
- segment_ids: int32 [16384, 12], P(('group', 'local')), may hold values from 0 to 255, as said below
- segment_count: int32 [16384], P(('group', 'local')), may hold values from 4 to 12
- gate_values: bfloat16 [16384, 12], P(('group', 'local')), may hold values from 0.099609375 to 1
- gate_weight: bfloat16 [256, 4096, 384], P(('group', 'local')), may hold values from -0.09375 to 0.09375
- up_weight: bfloat16 [256, 4096, 384], P(('group', 'local')), may hold values from -0.09375 to 0.09375
- down_weight: bfloat16 [256, 384, 4096], P(('group', 'local')), may hold values from -0.3125 to 0.3125
Outputs:
- mixed: bfloat16 [16384, 4096], P(('group', 'local'))
The draws below stay inside these ranges and needn't reach their ends.
Inputs may be any that keep to these rules, and one draw needn't show every extreme that they name: `segment_ids`: segment s is held by device s of the mesh and lies in group s // 16. A token's first segment_count entries are distinct and lie in exactly 4 groups with consecutive numbers modulo 16, one to three segments a group with consecutive local numbers modulo 16, listed group by group; later entries are not used. Of one device's tokens exactly 16 name segments of each group, and at most 3 name any one segment.
All inputs are finite; a program needn't handle non-finite values.
Results may differ from the reference program's by a relative error of at most 0.0064.
Values may be sent and summed in bfloat16 or wider, within the bound.
A program may use at most 128 MiB of HBM per device.

```python
import math
import jax
import jax.numpy as jnp
from jax import lax

D = 4096
SEG_W = 384
TOK_DEV = 64
GROUPS_TOK = 4
KMAX = 12
SEGMENTS = 256
TOKENS = 16384
CAP_G = 16
SEG_ROWS = 768
N_GROUP = 16
N_LOCAL = 16


def routing_draw(key):
    blocks = TOKENS // TOK_DEV
    per_group = TOK_DEV // N_GROUP
    key_perm, key_rotate, key_shuffle, key_picks = jax.random.split(key, 4)
    scores = jax.random.randint(key_perm, (blocks, TOK_DEV), 0, 65536) * TOK_DEV + jnp.arange(TOK_DEV, dtype=jnp.int32)[None, :]
    ranked = jnp.argsort(scores, axis=1).astype(jnp.int32)
    start_group = ranked % N_GROUP
    within = ranked // N_GROUP
    visit_steps = jnp.arange(GROUPS_TOK, dtype=jnp.int32)
    groups = (start_group[:, :, None] + visit_steps[None, None, :]) % N_GROUP
    visit = visit_steps[None, None, :] * per_group + within[:, :, None]
    rotate = jax.random.randint(key_rotate, (N_GROUP,), 0, N_LOCAL)
    scores_two = jax.random.randint(key_shuffle, (blocks, N_GROUP, CAP_G), 0, 65536) * CAP_G + jnp.arange(CAP_G, dtype=jnp.int32)[None, None, :]
    shuffled = jnp.argsort(scores_two, axis=2).astype(jnp.int32)
    block_index = jnp.arange(blocks, dtype=jnp.int32)[:, None, None]
    offset = shuffled[block_index, groups, visit] % N_LOCAL
    first_local = (rotate[groups] + offset) % N_LOCAL
    drawn = jax.random.randint(key_picks, (blocks, TOK_DEV, GROUPS_TOK), 1, 4)
    picks = jnp.where(offset == 0, 3, jnp.where(offset == 1, jnp.maximum(drawn, 2), drawn))
    picks = jnp.where((ranked == 0)[:, :, None], 3, picks).astype(jnp.int32)
    lanes = jnp.arange(3, dtype=jnp.int32)
    local_ids = (first_local[..., None] + lanes) % N_LOCAL
    named = groups[..., None] * N_LOCAL + local_ids
    alive = lanes < picks[..., None]
    before = jnp.cumsum(picks, axis=2) - picks
    target = jnp.where(alive, before[..., None] + lanes, KMAX)
    row_total = blocks * TOK_DEV
    named = named.reshape(row_total, GROUPS_TOK * 3).astype(jnp.int32)
    target = target.reshape(row_total, GROUPS_TOK * 3).astype(jnp.int32)
    row_index = jnp.arange(row_total, dtype=jnp.int32)[:, None]
    result = jnp.zeros((row_total, KMAX + 1), jnp.int32).at[row_index, target].set(named)[:, :KMAX]
    counted = jnp.sum(picks, axis=2).reshape(row_total).astype(jnp.int32)
    result = jnp.where(jnp.arange(KMAX, dtype=jnp.int32)[None, :] < counted[:, None], result, result[:, :1])
    return (result, counted)


def draw_segment_ids(key, part):
    result, counted = routing_draw(key)
    return result


def draw_segment_count(key, part):
    result, counted = routing_draw(key)
    return counted


def levels(own_key, dims, cuts, smallest, largest):
    gain = 1.0
    for axis_at, blocks in cuts:
        heights = jax.random.uniform(jax.random.fold_in(jax.random.fold_in(own_key, 6), axis_at), (blocks,), jnp.float32, smallest / len(cuts), largest / len(cuts))
        gain = gain * jnp.repeat(jnp.exp(heights), dims[axis_at] // blocks).reshape((-1,) + (1,) * (len(dims) - 1 - axis_at))
    return gain


def gaussian(own_key, shape, deviation, reach, cuts=(), kind=jnp.bfloat16):
    values = deviation * jax.random.normal(own_key, shape, jnp.float32)
    if cuts:
        values = values * levels(own_key, shape, cuts, -0.22, 0.18)
    return jnp.clip(values, -reach, reach).astype(kind)


def setup_inputs(seed: int = 0) -> dict:
    key_of = jax.random.split(jax.random.key(seed), 8)
    tokens = gaussian(key_of[0], (TOKENS, D), 1.0, 6.0, ((0, 256),))
    segment_ids = draw_segment_ids(jax.random.fold_in(key_of[7], 71), 0)
    segment_count = draw_segment_count(jax.random.fold_in(key_of[7], 71), 0)
    gate_values = jnp.clip(jnp.exp(math.log(1.0) - 2.306499 * jax.random.uniform(key_of[3], (TOKENS, KMAX), jnp.float32) ** levels(key_of[3], (TOKENS, KMAX), ((0, 256),), -0.2, 0.2)), 0.099609375, 1.0).astype(jnp.bfloat16)
    gate_weight = gaussian(key_of[4], (SEGMENTS, D, SEG_W), D ** -0.5, 0.09375, ((0, 256),))
    up_weight = gaussian(key_of[5], (SEGMENTS, D, SEG_W), D ** -0.5, 0.09375, ((0, 256),))
    down_weight = gaussian(key_of[6], (SEGMENTS, SEG_W, D), SEG_W ** -0.5, 0.3125, ((0, 256),))
    return dict(tokens=tokens, segment_ids=segment_ids, segment_count=segment_count, gate_values=gate_values, gate_weight=gate_weight, up_weight=up_weight, down_weight=down_weight)


def reference(tokens, segment_ids, segment_count, gate_values, gate_weight, up_weight, down_weight):
    slot_total = TOKENS * KMAX
    is_valid = lax.broadcasted_iota(jnp.int32, (TOKENS, KMAX), 1) < segment_count[:, None]
    flat_ids = jnp.where(is_valid, segment_ids, SEGMENTS).reshape(-1).astype(jnp.int32)
    flat_gate = jnp.where(is_valid, gate_values.astype(jnp.float32), 0.0).reshape(-1)
    flat_gate = jnp.concatenate([flat_gate, jnp.zeros((1,), jnp.float32)])
    owner_token = jnp.concatenate([jnp.arange(slot_total, dtype=jnp.int32) // KMAX, jnp.zeros((1,), jnp.int32)])
    sort_order = jnp.argsort(flat_ids, stable=True).astype(jnp.int32)
    sorted_ids = flat_ids[sort_order]
    counts = jax.ops.segment_sum(jnp.ones((slot_total,), jnp.int32), flat_ids, SEGMENTS + 1)
    starts = jnp.cumsum(counts) - counts
    places = jnp.arange(slot_total, dtype=jnp.int32) - starts[sorted_ids]
    seg_table = jnp.full((SEGMENTS + 1, SEG_ROWS), slot_total, jnp.int32)
    seg_table = seg_table.at[sorted_ids, places].set(sort_order, mode="drop")
    seg_table = seg_table[:SEGMENTS].reshape(N_GROUP, N_LOCAL, SEG_ROWS)
    gate_blocks = gate_weight.reshape(N_GROUP, N_LOCAL, D, SEG_W)
    up_blocks = up_weight.reshape(N_GROUP, N_LOCAL, D, SEG_W)
    down_blocks = down_weight.reshape(N_GROUP, N_LOCAL, SEG_W, D)

    def one_segment(partial_value, inputs):
        slot_rows, gate_block, up_block, down_block = inputs
        row_token = owner_token[slot_rows]
        row_gate = flat_gate[slot_rows]
        gathered = tokens[row_token]
        gated = jnp.dot(gathered, gate_block, preferred_element_type=jnp.float32)
        upward = jnp.dot(gathered, up_block, preferred_element_type=jnp.float32)
        hidden = (jax.nn.silu(gated) * upward).astype(jnp.bfloat16)
        output = jnp.dot(hidden, down_block, preferred_element_type=jnp.float32)
        weighted = lax.optimization_barrier((row_gate[:, None] * output).astype(jnp.bfloat16))
        return partial_value.at[row_token].add(weighted.astype(jnp.float32)), None

    def one_group(summed, inputs):
        partial_value, unused = lax.scan(one_segment, jnp.zeros((TOKENS, D), jnp.float32), inputs)
        rounded = lax.optimization_barrier(partial_value.astype(jnp.bfloat16))
        return summed + rounded.astype(jnp.float32), None

    summed, unused = lax.scan(one_group, jnp.zeros((TOKENS, D), jnp.float32), (seg_table, gate_blocks, up_blocks, down_blocks))
    return summed.astype(jnp.bfloat16)
```

```python
import functools

import jax
import jax.numpy as jnp
from jax import lax
from jax.experimental import pallas as pl
from jax.experimental.pallas import tpu as pltpu
from jax.sharding import PartitionSpec as P

MESH = pl.DeviceIdType.MESH
F32 = jnp.float32
BF16 = jnp.bfloat16

SETS = 4
ROWS = 16
SLOTS = 3
ORDERS = ((0, 1, 2, 3), (1, 0, 3, 2), (2, 3, 0, 1), (3, 2, 1, 0))


def dot(a, b):
    return jnp.dot(a, b, preferred_element_type=F32)


def dot_nt(a, b):
    return lax.dot_general(a, b, (((1,), (1,)), ((), ())), preferred_element_type=F32)


def iota(shape, dim):
    return lax.broadcasted_iota(jnp.int32, shape, dim)


def flip(value, bits):
    if bits == 1:
        return value + 1 - 2 * lax.rem(value, 2)
    if bits == 2:
        return 3 - value
    if bits == 3:
        return lax.rem(value + 2, 4)
    return value


def moved(local, bits):
    y, x = local // 4, lax.rem(local, 4)
    return flip(y, bits & 3) * 4 + flip(x, bits >> 2)


def kernel(
    groups,
    ids_ref, gates_ref, tok_ref, gate_hbm, up_hbm, down_hbm,
    out_ref,
    w_in, w_down, zs, zr, r1, p1, g3, s2, f1, acc, hid,
    take, give, meta_s, meta_r, meta_p, codes, sel, weigh, sel_tmp,
    w_sem, zm_send, zm_recv, pm_send, pm_recv,
    zd_send, zd_recv, zc_send, zc_recv,
    xd_send, xd_recv, xc_send, xc_recv,
):
    tokens = tok_ref.shape[0]
    width = hid.shape[1]
    cols = zs.shape[3]
    held = groups * ROWS
    pad = groups * SLOTS
    segments = groups * 16
    g = lax.axis_index("group")
    l = lax.axis_index("local")

    def rows_of(index):
        return pl.ds(pl.multiple_of(index * ROWS, ROWS), ROWS)

    def peer(j):
        return lax.rem(g + j, groups)

    barrier = pltpu.get_barrier_semaphore()

    def greet(j, carry):
        pl.semaphore_signal(barrier, inc=1, device_id=(peer(j), l), device_id_type=MESH)
        return carry

    lax.fori_loop(1, groups, greet, 0)
    for e in range(4):
        pl.semaphore_signal(barrier, inc=1, device_id=(g, moved(l, 1 << e)), device_id_type=MESH)

    weights = [
        pltpu.make_async_copy(gate_hbm.at[0], w_in.at[:, 0:width], w_sem.at[0]),
        pltpu.make_async_copy(up_hbm.at[0], w_in.at[:, width : 2 * width], w_sem.at[1]),
        pltpu.make_async_copy(down_hbm.at[0], w_down, w_sem.at[2]),
    ]
    for copy in weights:
        copy.start()

    ids = ids_ref[...]
    gates = gates_ref[...].astype(F32)
    label = iota((tokens, segments), 1)
    seg_gate = jnp.zeros((tokens, segments), F32)
    for k in range(ids.shape[1]):
        seg_gate += jnp.where(ids[:, k : k + 1] == label, gates[:, k : k + 1], 0.0)
    is_named = seg_gate > 0
    named = jnp.where(is_named, 1.0, 0.0).astype(BF16)
    in_group = jnp.where(iota((segments, 128), 0) // 16 == iota((segments, 128), 1), 1.0, 0.0).astype(BF16)
    in_group_t = jnp.where(iota((128, segments), 0) == iota((128, segments), 1) // 16, 1.0, 0.0).astype(BF16)
    square = (tokens, tokens)
    below = jnp.where(iota(square, 1) < iota(square, 0), 1.0, 0.0).astype(BF16)
    above = jnp.where(iota(square, 0) < iota(square, 1), 1.0, 0.0).astype(BF16)
    visit = dot(named, in_group) > 0
    place = jnp.where(visit, dot(below, jnp.where(visit, 1.0, 0.0).astype(BF16)), -1.0)
    give[...] = jnp.where(
        dot(place.astype(BF16), in_group_t) == (iota((tokens, held), 1) % ROWS).astype(F32), 1.0, 0.0
    ).astype(BF16)
    visit_t = dot_nt(in_group_t, named) > 0
    place_t = jnp.where(visit_t, dot(jnp.where(visit_t, 1.0, 0.0).astype(BF16), above), -1.0)
    take[...] = jnp.where(
        dot(in_group, place_t.astype(BF16)) == (iota((held, tokens), 0) % ROWS).astype(F32), 1.0, 0.0
    ).astype(BF16)
    rank = jnp.where(is_named, dot(below, named) + 1.0, 0.0).astype(BF16)
    own_group = iota((held, segments), 0) // ROWS == iota((held, segments), 1) // 16
    fold = jnp.where(iota((segments, 128), 0) % 16 == iota((segments, 128), 1), 1.0, 0.0).astype(BF16)
    fold_far = jnp.where(iota((segments, 128), 0) % 16 + 16 == iota((segments, 128), 1), 1.0, 0.0).astype(BF16)
    ranks = jnp.where(own_group, dot(take[...], rank), 0.0).astype(BF16)
    row_gates = jnp.where(own_group, dot(take[...], seg_gate.astype(BF16)), 0.0).astype(BF16)
    meta_s[...] = (dot(ranks, fold) + dot(row_gates, fold_far)).astype(BF16)

    def gather(k):
        for v in range(4):
            part = tok_ref[:, (4 * k + v) * cols : (4 * k + v + 1) * cols]
            zs[k, v] = dot(take[...], part).astype(BF16)

    gather(0)
    pl.semaphore_wait(barrier, groups - 1 + 4)

    def meta_copy(j):
        return pltpu.make_async_remote_copy(
            src_ref=meta_s.at[rows_of(peer(j))], dst_ref=meta_r.at[rows_of(g)],
            send_sem=zm_send.at[j], recv_sem=zm_recv.at[j],
            device_id=(peer(j), l), device_id_type=MESH,
        )

    def out_copy(k, j):
        return pltpu.make_async_remote_copy(
            src_ref=zs.at[k, :, rows_of(peer(j)), :], dst_ref=zr.at[k, :, rows_of(g), :],
            send_sem=zd_send.at[k, j], recv_sem=zd_recv.at[k, j],
            device_id=(peer(j), l), device_id_type=MESH,
        )

    def back_copy(k, j):
        return pltpu.make_async_remote_copy(
            src_ref=zr.at[k, :, rows_of(peer(j)), :], dst_ref=zs.at[k, :, rows_of(g), :],
            send_sem=zc_send.at[k, j], recv_sem=zc_recv.at[k, j],
            device_id=(peer(j), l), device_id_type=MESH,
        )

    def start_all(make):
        def body(j, carry):
            make(j).start()
            return carry

        lax.fori_loop(1, groups, body, 0)

    def wait_all(make):
        def body(j, carry):
            make(j).wait()
            return carry

        lax.fori_loop(1, groups, body, 0)

    def start_out(k):
        start_all(functools.partial(out_copy, k))

    def exchange(e, src, dst, send, recv):
        return pltpu.make_async_remote_copy(
            src_ref=src, dst_ref=dst, send_sem=send, recv_sem=recv,
            device_id=(g, moved(l, 1 << e)), device_id_type=MESH,
        )

    def forth(k, v, step):
        kv = k * 4 + v
        src, dst = (
            (zr.at[k, v], r1.at[kv]),
            (s2.at[kv], g3.at[kv, 0:2, :, 1]),
            (g3.at[kv, 0], g3.at[kv, 2]),
            (g3.at[kv, 1:3, 1], f1.at[kv]),
        )[step]
        return exchange(ORDERS[v][step], src, dst, xd_send.at[step, kv], xd_recv.at[step, kv])

    def back(k, v, step):
        kv = k * 4 + v
        src, dst = (
            (r1.at[kv], p1.at[kv]),
            (g3.at[kv, 0:2, :, 1], s2.at[kv]),
            (g3.at[kv, 2], g3.at[kv, 0]),
            (f1.at[kv], g3.at[kv, 1:3, 1]),
        )[step]
        return exchange(ORDERS[v][step], src, dst, xc_send.at[step, kv], xc_recv.at[step, kv])

    def partner_meta(e):
        return exchange(e, meta_r, meta_p.at[e], pm_send.at[e], pm_recv.at[e])

    start_all(meta_copy)
    start_out(0)
    gather(1)
    start_out(1)
    for k in range(2, SETS):
        gather(k)
    meta_r[rows_of(g), :] = meta_s[rows_of(g), :]
    wait_all(meta_copy)
    for e in range(4):
        partner_meta(e).start()

    eye = jnp.where(iota((128, 128), 0) == iota((128, 128), 1), 1.0, 0.0).astype(BF16)
    eye_held = jnp.where(iota((held, held), 0) == iota((held, held), 1), 1.0, 0.0).astype(BF16)
    base = (iota((16, held), 1) // ROWS * SLOTS - 1).astype(F32)
    slot = iota((pad, held), 0).astype(F32)

    def decode(index, meta):
        turned = dot_nt(eye, meta)
        codes[index, 0:16] = jnp.where(turned[0:16] > 0, base + turned[0:16], -1.0)
        codes[index, 16:32] = turned[16:32]

    def build(v, r):
        e1, e2, e3, e4 = ORDERS[v]
        index = 1 + e1 if r else 0
        for d2 in range(2):
            for q in range(2):
                for d4 in range(2):
                    place = moved(l, d2 << e2 | (1 - q) << e3 | d4 << e4)
                    b = (d2 * 2 + q) * 2 + d4
                    hit = slot == codes[index, pl.ds(place, 1), :]
                    sel[v, r, b * pad : (b + 1) * pad, :] = jnp.where(hit, 1.0, 0.0).astype(BF16)
                    sel_tmp[b * pad : (b + 1) * pad, :] = jnp.where(
                        hit, codes[index, pl.ds(place + 16, 1), :], 0.0
                    ).astype(BF16)
        weigh[v, r] = dot_nt(eye_held, sel_tmp[...]).astype(BF16)

    decode(0, meta_r[...])
    for v in range(4):
        build(v, 0)
    for e in range(4):
        partner_meta(e).wait()
        decode(1 + e, meta_p[e])
    for v in range(4):
        build(v, 1)

    acc[...] = jnp.zeros_like(acc)
    for copy in weights:
        copy.wait()

    def select(k, v, r, rows):
        kv = k * 4 + v
        chosen = dot(sel[v, r], rows).astype(BF16)
        for q in range(2):
            for d4 in range(2):
                b = q * 2 + d4
                g3[kv, q, d4, 0, r * pad : (r + 1) * pad, :] = chosen[b * pad : (b + 1) * pad]
                b += 4
                s2[kv, q, d4, r * pad : (r + 1) * pad, :] = chosen[b * pad : (b + 1) * pad]

    def block_of(v, r4, r3, r2, r1_):
        e1, e2, e3, e4 = ORDERS[v]
        return r4 << e4 | r3 << e3 | r2 << e2 | r1_ << e1

    def accumulate(k, v, r4, rows):
        at = pl.ds(pl.multiple_of((k * 4 + v) * cols, cols), cols)
        part = dot(rows.reshape(8 * pad, cols), w_in[at, :])
        for b in range(8):
            c = block_of(v, r4, b >> 2, b >> 1 & 1, b & 1)
            acc[c] += part[b * pad : (b + 1) * pad]

    def forth_a(k):
        for v in range(4):
            zr[k, v, rows_of(g), :] = zs[k, v, rows_of(g), :]
        wait_all(functools.partial(out_copy, k))
        for v in range(4):
            forth(k, v, 0).start()

        @pl.when(k + 2 < SETS)
        def _():
            start_out(k + 2)

        for v in range(4):
            select(k, v, 0, zr[k, v])

    def forth_b(k):
        for v in range(4):
            forth(k, v, 0).wait()
            select(k, v, 1, r1[k * 4 + v])
            forth(k, v, 1).start()

    def forth_c(k):
        for v in range(4):
            forth(k, v, 1).wait()
            forth(k, v, 2).start()

    def forth_d(k):
        for v in range(4):
            forth(k, v, 2).wait()
            forth(k, v, 3).start()
        for v in range(4):
            accumulate(k, v, 0, g3[k * 4 + v, 1:3, 0])

    def forth_e(k):
        for v in range(4):
            forth(k, v, 3).wait()
            accumulate(k, v, 1, f1[k * 4 + v])

    def pipeline(stages):
        depth = len(stages)

        def body(t, carry):
            for lag in range(depth - 1, -1, -1):
                k = t - lag

                @pl.when((k >= 0) & (k < SETS))
                def _(stage=stages[lag], k=k):
                    stage(k)

            return carry

        lax.fori_loop(0, SETS + depth - 1, body, 0)

    pipeline((forth_a, forth_b, forth_c, forth_d, forth_e))

    for c in range(16):
        gated = acc[c, :, 0:width]
        upward = acc[c, :, width : 2 * width]
        hid[c * pad : (c + 1) * pad, :] = (gated / (1.0 + jnp.exp(-gated)) * upward).astype(BF16)

    def back_a(k):
        for v in range(4):
            kv = k * 4 + v
            at = pl.ds(pl.multiple_of(kv * cols, cols), cols)
            result = dot(hid[...], w_down[:, at]).astype(BF16)
            for b in range(8):
                r3, r2, r1_ = b >> 2, b >> 1 & 1, b & 1
                inner = slice(r1_ * pad, (r1_ + 1) * pad)
                c = block_of(v, 1, r3, r2, r1_)
                f1[kv, r3, r2, inner, :] = result[c * pad : (c + 1) * pad]
                c = block_of(v, 0, r3, r2, r1_)
                g3[kv, 1 + r3, 0, r2, inner, :] = result[c * pad : (c + 1) * pad]
            back(k, v, 3).start()

    def back_b(k):
        for v in range(4):
            back(k, v, 3).wait()
            back(k, v, 2).start()

    def back_c(k):
        for v in range(4):
            back(k, v, 2).wait()
            back(k, v, 1).start()

    def part_sum(k, v, r):
        kv = k * 4 + v
        inner = slice(r * pad, (r + 1) * pad)
        near = g3[kv, 0:2, :, 0, inner, :].reshape(4 * pad, cols)
        far = s2[kv, :, :, inner, :].reshape(4 * pad, cols)
        return dot(weigh[v, r], jnp.concatenate([near, far], axis=0))

    def back_d(k):
        for v in range(4):
            back(k, v, 1).wait()
            r1[k * 4 + v] = part_sum(k, v, 1).astype(BF16)
            back(k, v, 0).start()

    def back_e(k):
        for v in range(4):
            own = part_sum(k, v, 0)
            back(k, v, 0).wait()
            zr[k, v] = (own + p1[k * 4 + v].astype(F32)).astype(BF16)
        start_all(functools.partial(back_copy, k))
        for v in range(4):
            zs[k, v, rows_of(g), :] = zr[k, v, rows_of(g), :]

    def back_f(k):
        wait_all(functools.partial(back_copy, k))
        for v in range(4):
            at = pl.ds(pl.multiple_of((k * 4 + v) * cols, cols), cols)
            out_ref[:, at] = dot(give[...], zs[k, v]).astype(BF16)

    pipeline((back_a, back_b, back_c, back_d, back_e, back_f))


def on_device(tokens, segment_ids, segment_count, gate_values, gate_weight, up_weight, down_weight):
    groups = lax.axis_size("group")
    model = tokens.shape[1]
    width = gate_weight.shape[2]
    cols = model // (4 * SETS)
    held = groups * ROWS
    pad = groups * SLOTS
    is_valid = lax.broadcasted_iota(jnp.int32, segment_ids.shape, 1) < segment_count[:, None]
    ids = jnp.where(is_valid, segment_ids, -1)
    vmem = pl.BlockSpec(memory_space=pltpu.VMEM)
    hbm = pl.BlockSpec(memory_space=pl.ANY)
    dma = pltpu.SemaphoreType.DMA
    return pl.pallas_call(
        functools.partial(kernel, groups),
        out_shape=jax.ShapeDtypeStruct(tokens.shape, BF16),
        in_specs=[vmem, vmem, vmem, hbm, hbm, hbm],
        out_specs=vmem,
        scratch_shapes=[
            pltpu.VMEM((model, 2 * width), BF16),
            pltpu.VMEM((width, model), BF16),
            pltpu.VMEM((SETS, 4, held, cols), BF16),
            pltpu.VMEM((SETS, 4, held, cols), BF16),
            pltpu.VMEM((SETS * 4, held, cols), BF16),
            pltpu.VMEM((SETS * 4, held, cols), BF16),
            pltpu.VMEM((SETS * 4, 3, 2, 2, 2 * pad, cols), BF16),
            pltpu.VMEM((SETS * 4, 2, 2, 2 * pad, cols), BF16),
            pltpu.VMEM((SETS * 4, 2, 2, 2 * pad, cols), BF16),
            pltpu.VMEM((16, pad, 2 * width), F32),
            pltpu.VMEM((16 * pad, width), BF16),
            pltpu.VMEM((held, tokens.shape[0]), BF16),
            pltpu.VMEM((tokens.shape[0], held), BF16),
            pltpu.VMEM((held, 128), BF16),
            pltpu.VMEM((held, 128), BF16),
            pltpu.VMEM((4, held, 128), BF16),
            pltpu.VMEM((5, 32, held), F32),
            pltpu.VMEM((4, 2, 8 * pad, held), BF16),
            pltpu.VMEM((4, 2, held, 8 * pad), BF16),
            pltpu.VMEM((8 * pad, held), BF16),
            dma((3,)),
            dma((groups,)), dma((groups,)), dma((4,)), dma((4,)),
            dma((SETS, groups)), dma((SETS, groups)), dma((SETS, groups)), dma((SETS, groups)),
            dma((4, SETS * 4)), dma((4, SETS * 4)), dma((4, SETS * 4)), dma((4, SETS * 4)),
        ],
        compiler_params=pltpu.CompilerParams(
            collective_id=0, has_side_effects=True, vmem_limit_bytes=56 * 1024 * 1024
        ),
    )(ids, gate_values, tokens, gate_weight, up_weight, down_weight)


def solution(mesh):
    return jax.shard_map(
        on_device,
        mesh=mesh,
        in_specs=(
            P(("group", "local"), None),
            P(("group", "local"), None),
            P(("group", "local")),
            P(("group", "local"), None),
            P(("group", "local"), None, None),
            P(("group", "local"), None, None),
            P(("group", "local"), None, None),
        ),
        out_specs=P(("group", "local"), None),
        check_vma=False,
    )
```

```python
import functools

import jax
import jax.numpy as jnp
from jax import lax
from jax.experimental import pallas as pl
from jax.experimental.pallas import tpu as pltpu
from jax.sharding import PartitionSpec as P

MESH = pl.DeviceIdType.MESH
F32 = jnp.float32
BF16 = jnp.bfloat16

WIDTHS = (128,) * 8
SETS = tuple(tuple((v, width) for v in range(4)) for width in WIDTHS)
ROWS = 16
SLOTS = 3
ORDERS = ((0, 1, 2, 3), (1, 0, 3, 2), (2, 3, 0, 1), (3, 2, 1, 0))


FORTH = (
    (0, 0), (1, 0), (1, 1), (1, 2), (1, 3), (2, 0), (2, 1), (2, 2), (2, 3), (3, 0), (3, 1), (3, 2), (3, 3), (0,
    1), (1, 4), (1, 5), (1, 6), (1, 7), (2, 4), (2, 5), (2, 6), (2, 7), (4, 0), (4, 1), (4, 2), (4, 3), (3, 5),
    (3, 4), (3, 7), (3, 6), (0, 2), (1, 8), (1, 9), (1, 10), (1, 11), (2, 8), (2, 9), (5, 1), (2, 10), (5, 0),
    (5, 2), (2, 11), (5, 3), (6, 0), (6, 1), (6, 2), (6, 3), (4, 5), (4, 6), (4, 7), (4, 4), (3, 10), (3, 8),
    (3, 9), (3, 11), (0, 3), (1, 12), (1, 13), (1, 14), (1, 15), (2, 12), (2, 13), (2, 14), (2, 15), (7, 0), (7,
    1), (5, 4), (5, 5), (5, 6), (7, 2), (5, 7), (7, 3), (0, 4), (1, 16), (1, 17), (1, 18), (1, 19), (4, 9), (4,
    10), (4, 8), (4, 11), (2, 16), (2, 17), (3, 14), (3, 12), (3, 13), (3, 15), (2, 18), (2, 19), (7, 5), (7,
    4), (7, 6), (7, 7), (3, 18), (3, 16), (3, 17), (3, 19), (0, 5), (5, 8), (5, 9), (5, 10), (5, 11), (1, 20),
    (1, 21), (1, 22), (1, 23), (2, 20), (2, 21), (2, 22), (2, 23), (4, 15), (4, 13), (4, 14), (6, 4), (4, 12),
    (6, 5), (6, 6), (0, 6), (1, 24), (1, 25), (1, 26), (1, 27), (4, 16), (4, 17), (4, 18), (4, 19), (2, 24), (2,
    25), (2, 26), (2, 27), (7, 9), (7, 8), (7, 10), (7, 11), (3, 20), (3, 21), (3, 22), (3, 23), (0, 7), (5,
    12), (5, 13), (5, 14), (5, 15), (1, 28), (1, 29), (1, 30), (1, 31), (2, 28), (3, 26), (3, 24), (3, 25), (3,
    27), (2, 29), (2, 30), (5, 16), (5, 17), (5, 18), (2, 31), (5, 19), (6, 7), (6, 8), (6, 9), (6, 10), (4,
    21), (4, 22), (4, 23), (4, 20), (6, 11), (6, 12), (6, 13), (6, 14), (7, 12), (7, 13), (7, 14), (3, 30), (3,
    28), (3, 29), (3, 31), (7, 15), (4, 27), (6, 15), (4, 25), (4, 26), (4, 24), (6, 16), (6, 17), (6, 18), (6,
    19), (7, 16), (7, 17), (7, 18), (7, 19), (5, 20), (6, 20), (5, 21), (5, 22), (5, 23), (6, 21), (6, 22), (6,
    23), (4, 31), (4, 29), (4, 30), (4, 28), (5, 24), (6, 24), (5, 25), (5, 26), (5, 27), (6, 25), (6, 26), (6,
    27), (7, 21), (7, 20), (7, 22), (7, 23), (5, 28), (6, 28), (5, 29), (5, 30), (5, 31), (6, 29), (6, 30), (6,
    31), (7, 25), (7, 24), (7, 26), (7, 27), (7, 28), (7, 29), (7, 30), (7, 31),
)


def dot(a, b):
    return jnp.dot(a, b, preferred_element_type=F32)


def dot_nt(a, b):
    return lax.dot_general(a, b, (((1,), (1,)), ((), ())), preferred_element_type=F32)


def iota(shape, dim):
    return lax.broadcasted_iota(jnp.int32, shape, dim)


def flip(value, bits):
    if bits == 1:
        return value + 1 - 2 * lax.rem(value, 2)
    if bits == 2:
        return 3 - value
    if bits == 3:
        return lax.rem(value + 2, 4)
    return value


def moved(local, bits):
    y, x = local // 4, lax.rem(local, 4)
    return flip(y, bits & 3) * 4 + flip(x, bits >> 2)


def one(mask):
    return jnp.where(mask, 1.0, 0.0).astype(BF16)


def kernel(
    groups,
    order,
    ids_ref, count_ref, gates_ref, tok_ref, gate_hbm, up_hbm, down_hbm,
    out_ref,
    w_in, w_down, acc, hid,
    take, give, meta_s, meta_r, meta_p, codes, sel, weigh, sel_tmp,
    w_sem, zm_send, zm_recv, pm_send, pm_recv,
    zd_send, zd_recv, zc_send, zc_recv,
    xd_send, xd_recv, xc_send, xc_recv,
    *buffers,
):
    sets, items = layout()
    zs, zr = buffers[: len(sets)], buffers[len(sets) : 2 * len(sets)]
    zb = buffers[2 * len(sets) : 3 * len(sets)]
    r1, p1, g3, s2, f1 = (
        buffers[3 * len(sets) + n * len(items) : 3 * len(sets) + (n + 1) * len(items)] for n in range(5)
    )
    tokens = tok_ref.shape[0]
    width = hid.shape[1]
    held = groups * ROWS
    pad = groups * SLOTS
    segments = groups * 16
    g = lax.axis_index("group")
    l = lax.axis_index("local")

    def rows_of(index):
        return pl.ds(pl.multiple_of(index * ROWS, ROWS), ROWS)

    def peer(j):
        return lax.rem(g + j, groups)

    barrier = pltpu.get_barrier_semaphore()

    def greet(j, carry):
        pl.semaphore_signal(barrier, inc=1, device_id=(peer(j), l), device_id_type=MESH)
        return carry

    lax.fori_loop(1, groups, greet, 0)
    for e in range(4):
        pl.semaphore_signal(barrier, inc=1, device_id=(g, moved(l, 1 << e)), device_id_type=MESH)

    weights = [
        pltpu.make_async_copy(gate_hbm.at[0], w_in.at[:, 0:width], w_sem.at[0]),
        pltpu.make_async_copy(up_hbm.at[0], w_in.at[:, width : 2 * width], w_sem.at[1]),
        pltpu.make_async_copy(down_hbm.at[0], w_down, w_sem.at[2]),
    ]
    for copy in weights:
        copy.start()

    ids = jnp.where(iota(ids_ref.shape, 0) < count_ref[...], ids_ref[...], -1)
    gates = gates_ref[...].astype(F32)
    label = iota((segments, tokens), 0)
    seg_gate = jnp.zeros((segments, tokens), F32)
    for k in range(ids.shape[0]):
        seg_gate += jnp.where(ids[k : k + 1] == label, gates[k : k + 1], 0.0)
    is_named = seg_gate > 0
    named = one(is_named)
    in_group = one(iota((segments, 128), 0) // 16 == iota((segments, 128), 1))
    in_group_t = one(iota((128, segments), 0) == iota((128, segments), 1) // 16)
    earlier = one(iota((tokens, tokens), 0) < iota((tokens, tokens), 1))
    visit = dot(in_group_t, named) > 0
    place = jnp.where(visit, dot(one(visit), earlier), -1.0)
    take[...] = one(dot(in_group, place.astype(BF16)) == (iota((held, tokens), 0) % ROWS).astype(F32))
    rank = jnp.where(is_named, dot(named, earlier) + 1.0, 0.0).astype(BF16)
    own_group = iota((held, segments), 0) // ROWS == iota((held, segments), 1) // 16
    fold = one(iota((segments, 128), 0) % 16 == iota((segments, 128), 1))
    fold_far = one(iota((segments, 128), 0) % 16 + 16 == iota((segments, 128), 1))
    ranks = jnp.where(own_group, dot_nt(take[...], rank), 0.0).astype(BF16)
    row_gates = jnp.where(own_group, dot_nt(take[...], seg_gate.astype(BF16)), 0.0).astype(BF16)
    meta_s[...] = (dot(ranks, fold) + dot(row_gates, fold_far)).astype(BF16)

    def gather(k):
        base, wide, _ = sets[k]
        zs[k][...] = dot(take[...], tok_ref[:, base : base + wide]).astype(BF16)

    for k in range(len(sets)):
        gather(k)
    acc[...] = jnp.zeros_like(acc)
    eye = one(iota((128, 128), 0) == iota((128, 128), 1))
    eye_held = one(iota((held, held), 0) == iota((held, held), 1))
    eye_tokens = one(iota((tokens, tokens), 0) == iota((tokens, tokens), 1))
    give[...] = dot_nt(eye_tokens, take[...]).astype(BF16)
    meta_r[rows_of(g), :] = meta_s[rows_of(g), :]
    for copy in weights:
        copy.wait()
    pl.semaphore_wait(barrier, groups - 1 + 4)

    def meta_copy(j):
        return pltpu.make_async_remote_copy(
            src_ref=meta_s.at[rows_of(peer(j))], dst_ref=meta_r.at[rows_of(g)],
            send_sem=zm_send.at[j], recv_sem=zm_recv.at[j],
            device_id=(peer(j), l), device_id_type=MESH,
        )

    def out_copy(k, j):
        return pltpu.make_async_remote_copy(
            src_ref=zs[k].at[rows_of(peer(j)), :], dst_ref=zr[k].at[rows_of(g), :],
            send_sem=zd_send.at[k, j], recv_sem=zd_recv.at[k, j],
            device_id=(peer(j), l), device_id_type=MESH,
        )

    def back_copy(k, j):
        return pltpu.make_async_remote_copy(
            src_ref=zr[k].at[rows_of(peer(j)), :], dst_ref=zb[k].at[rows_of(g), :],
            send_sem=zc_send.at[k, j], recv_sem=zc_recv.at[k, j],
            device_id=(peer(j), l), device_id_type=MESH,
        )

    def start_all(make):
        def body(j, carry):
            make(j).start()
            return carry

        lax.fori_loop(1, groups, body, 0)

    def wait_all(make):
        def body(j, carry):
            make(j).wait()
            return carry

        lax.fori_loop(1, groups, body, 0)

    def start_out(k):
        start_all(functools.partial(out_copy, k))

    def exchange(e, src, dst, send, recv):
        return pltpu.make_async_remote_copy(
            src_ref=src, dst_ref=dst, send_sem=send, recv_sem=recv,
            device_id=(g, moved(l, 1 << e)), device_id_type=MESH,
        )

    def forth(i, step):
        k, off, wide, v = items[i]
        src, dst = (
            (zr[k].at[:, off : off + wide], r1[i]),
            (s2[i], g3[i].at[0:2, :, 1]),
            (g3[i].at[0], g3[i].at[2]),
            (g3[i].at[1:3, 1], f1[i]),
        )[step]
        return exchange(ORDERS[v][step], src, dst, xd_send.at[step, i], xd_recv.at[step, i])

    def back(i, step):
        v = items[i][3]
        src, dst = (
            (r1[i], p1[i]),
            (g3[i].at[0:2, :, 1], s2[i]),
            (g3[i].at[2], g3[i].at[0]),
            (f1[i], g3[i].at[1:3, 1]),
        )[step]
        return exchange(ORDERS[v][step], src, dst, xc_send.at[step, i], xc_recv.at[step, i])

    def partner_meta(e):
        return exchange(e, meta_r, meta_p.at[e], pm_send.at[e], pm_recv.at[e])

    start_all(meta_copy)
    start_out(0)
    start_out(1)
    wait_all(meta_copy)
    for e in range(4):
        partner_meta(e).start()
    for k in range(2, len(sets)):
        start_out(k)

    first = (iota((16, held), 1) // ROWS * SLOTS - 1).astype(F32)
    slot = iota((pad, held), 0).astype(F32)

    def decode(index, meta):
        turned = dot_nt(eye, meta)
        codes[index, 0:16] = jnp.where(turned[0:16] > 0, first + turned[0:16], -1.0)
        codes[index, 16:32] = turned[16:32]

    def hits(v, r):
        e1, e2, e3, e4 = ORDERS[v]
        index = 1 + e1 if r else 0
        for b in range(8):
            d2, q, d4 = b >> 2, b >> 1 & 1, b & 1
            segment = moved(l, d2 << e2 | (1 - q) << e3 | d4 << e4)
            hit = slot == codes[index, pl.ds(segment, 1), :]
            yield slice(b * pad, (b + 1) * pad), hit, codes[index, pl.ds(segment + 16, 1), :]

    def build_sel(v, r):
        for at, hit, _ in hits(v, r):
            sel[v, r, at, :] = one(hit)

    def build_weigh(v, r):
        for at, hit, gate in hits(v, r):
            sel_tmp[at, :] = jnp.where(hit, gate, 0.0).astype(BF16)
        weigh[v, r] = dot_nt(eye_held, sel_tmp[...]).astype(BF16)

    decode(0, meta_r[...])
    for v in range(4):
        build_sel(v, 0)

    def partners(_):
        for e in range(4):
            partner_meta(e).wait()
            decode(1 + e, meta_p[e])
        for v in range(4):
            build_sel(v, 1)

    def select(i, r, rows):
        chosen = dot(sel[items[i][3], r], rows).astype(BF16)
        inner = slice(r * pad, (r + 1) * pad)
        for b in range(4):
            q, d4 = b >> 1, b & 1
            s2[i][q, d4, inner, :] = chosen[(4 + b) * pad : (5 + b) * pad]
            g3[i][q, d4, 0, inner, :] = chosen[b * pad : (b + 1) * pad]

    def block_of(v, r4, b):
        e1, e2, e3, e4 = ORDERS[v]
        return r4 << e4 | (b >> 2) << e3 | (b >> 1 & 1) << e2 | (b & 1) << e1

    def accumulate(i, r4, rows):
        k, off, wide, v = items[i]
        base = sets[k][0] + off
        part = dot(rows.reshape(8 * pad, wide), w_in[base : base + wide, :])
        for b in range(8):
            acc[block_of(v, r4, b)] += part[b * pad : (b + 1) * pad]

    def forth_z(k):
        zr[k][rows_of(g), :] = zs[k][rows_of(g), :]
        wait_all(functools.partial(out_copy, k))

    def forth_0(i):
        forth(i, 0).start()

    def forth_own(i):
        k, off, wide, v = items[i]
        select(i, 0, zr[k][:, off : off + wide])

    def forth_1(i):
        forth(i, 0).wait()
        select(i, 1, r1[i][...])
        forth(i, 1).start()

    def forth_2(i):
        forth(i, 1).wait()
        forth(i, 2).start()

    def forth_3(i):
        forth(i, 2).wait()
        forth(i, 3).start()

    def forth_near(i):
        accumulate(i, 0, g3[i][1:3, 0])

    def forth_far(i):
        forth(i, 3).wait()
        accumulate(i, 1, f1[i][...])

    def weights_back(v):
        for r in range(2):
            build_weigh(v, r)

    def activate(_):
        for c in range(16):
            gated = acc[c, :, 0:width]
            upward = acc[c, :, width : 2 * width]
            hid[c * pad : (c + 1) * pad, :] = (gated / (1.0 + jnp.exp(-gated)) * upward).astype(BF16)

    def back_3(i):
        k, off, wide, v = items[i]
        base = sets[k][0] + off
        result = dot(hid[...], w_down[:, base : base + wide]).astype(BF16)
        for r4 in (1, 0):
            for b in range(8):
                r3, r2, r1_ = b >> 2, b >> 1 & 1, b & 1
                inner = slice(r1_ * pad, (r1_ + 1) * pad)
                c = block_of(v, r4, b)
                if r4:
                    f1[i][r3, r2, inner, :] = result[c * pad : (c + 1) * pad]
                else:
                    g3[i][1 + r3, 0, r2, inner, :] = result[c * pad : (c + 1) * pad]
            if r4:
                back(i, 3).start()

    def back_2(i):
        back(i, 3).wait()
        back(i, 2).start()

    def back_1(i):
        back(i, 2).wait()
        back(i, 1).start()

    def part_sum(i, r):
        k, off, wide, v = items[i]
        inner = slice(r * pad, (r + 1) * pad)
        near = g3[i][0:2, :, 0, inner, :].reshape(4 * pad, wide)
        far = s2[i][:, :, inner, :].reshape(4 * pad, wide)
        return dot(weigh[v, r], jnp.concatenate([near, far], axis=0))

    def back_0(i):
        back(i, 1).wait()
        r1[i][...] = part_sum(i, 1).astype(BF16)
        back(i, 0).start()

    def back_own(i):
        k, off, wide, v = items[i]
        own = part_sum(i, 0)
        back(i, 0).wait()
        zr[k][:, off : off + wide] = (own + p1[i][...].astype(F32)).astype(BF16)

    def back_z(k):
        start_all(functools.partial(back_copy, k))
        zb[k][rows_of(g), :] = zr[k][rows_of(g), :]

    def back_out(k):
        base, wide, _ = sets[k]
        wait_all(functools.partial(back_copy, k))
        out_ref[:, base : base + wide] = dot(give[...], zb[k][...]).astype(BF16)

    steps = (
        forth_z, forth_0, forth_own, forth_1, forth_2, forth_3, forth_near, forth_far,
        weights_back, partners, activate,
        back_3, back_2, back_1, back_0, back_own, back_z, back_out,
    )
    for step, index in order:
        steps[step](index)


def layout():
    sets, items, base = [], [], 0
    for k, members in enumerate(SETS):
        offset, inside = 0, []
        for v, wide in members:
            inside.append(len(items))
            items.append((k, offset, wide, v))
            offset += wide
        sets.append((base, offset, inside))
        base += offset
    return sets, items


def program_order():
    sets, items = layout()
    count = len(sets)
    order = []

    def slots(sequence, stages):
        depth = 1 + max(lag for lag, _, _ in stages)
        for t in range(count + depth - 1):
            for lag, step, whole in stages:
                if 0 <= t - lag < count:
                    k = sequence[t - lag]
                    for index in (k,) if whole else sets[k][2]:
                        for s in step:
                            order.append((s, index))

    order.extend(FORTH)
    order.append((10, 0))
    slots(range(count), (
        (4, (15,), False), (4, (16,), True), (3, (14,), False), (2, (13,), False), (1, (12,), False), (0, (11,), False),
        (5, (17,), True),
    ))
    place = next(n for n, (s, _) in enumerate(order) if s == 3)
    order.insert(place, (9, 0))
    place = next(n for n, (s, _) in enumerate(order) if s == 7)
    return order[:place] + [(8, v) for v in range(4)] + order[place:]


def on_device(tokens, segment_ids, segment_count, gate_values, gate_weight, up_weight, down_weight):
    groups = lax.axis_size("group")
    model = tokens.shape[1]
    width = gate_weight.shape[2]
    held = groups * ROWS
    pad = groups * SLOTS
    sets, items = layout()
    n_sets, n_items = len(sets), len(items)
    vmem = pl.BlockSpec(memory_space=pltpu.VMEM)
    hbm = pl.BlockSpec(memory_space=pl.ANY)
    dma = pltpu.SemaphoreType.DMA

    def per_set():
        return [pltpu.VMEM((held, wide), BF16) for _, wide, _ in sets]

    def per_item(*shape):
        return [pltpu.VMEM(shape + (wide,), BF16) for _, _, wide, _ in items]

    return pl.pallas_call(
        functools.partial(kernel, groups, program_order()),
        out_shape=jax.ShapeDtypeStruct(tokens.shape, BF16),
        in_specs=[vmem, vmem, vmem, vmem, hbm, hbm, hbm],
        out_specs=vmem,
        scratch_shapes=[
            pltpu.VMEM((model, 2 * width), BF16),
            pltpu.VMEM((width, model), BF16),
            pltpu.VMEM((16, pad, 2 * width), F32),
            pltpu.VMEM((16 * pad, width), BF16),
            pltpu.VMEM((held, tokens.shape[0]), BF16),
            pltpu.VMEM((tokens.shape[0], held), BF16),
            pltpu.VMEM((held, 128), BF16),
            pltpu.VMEM((held, 128), BF16),
            pltpu.VMEM((4, held, 128), BF16),
            pltpu.VMEM((5, 32, held), F32),
            pltpu.VMEM((4, 2, 8 * pad, held), BF16),
            pltpu.VMEM((4, 2, held, 8 * pad), BF16),
            pltpu.VMEM((8 * pad, held), BF16),
            dma((3,)),
            dma((groups,)), dma((groups,)), dma((4,)), dma((4,)),
            *[dma((n_sets, groups))] * 4,
            *[dma((4, n_items))] * 4,
            *per_set(), *per_set(), *per_set(),
            *per_item(held), *per_item(held),
            *per_item(3, 2, 2, 2 * pad),
            *per_item(2, 2, 2 * pad), *per_item(2, 2, 2 * pad),
        ],
        compiler_params=pltpu.CompilerParams(
            collective_id=0, has_side_effects=True, vmem_limit_bytes=56 * 1024 * 1024
        ),
    )(segment_ids.T, segment_count[None, :], gate_values.T, tokens, gate_weight, up_weight, down_weight)


def solution(mesh):
    return jax.shard_map(
        on_device,
        mesh=mesh,
        in_specs=(
            P(("group", "local"), None),
            P(("group", "local"), None),
            P(("group", "local")),
            P(("group", "local"), None),
            P(("group", "local"), None, None),
            P(("group", "local"), None, None),
            P(("group", "local"), None, None),
        ),
        out_specs=P(("group", "local"), None),
        check_vma=False,
    )
```

```python
import functools

import jax
import jax.numpy as jnp
from jax import lax
from jax.experimental import pallas as pl
from jax.experimental.pallas import tpu as pltpu
from jax.sharding import PartitionSpec as P

MESH = pl.DeviceIdType.MESH
F32 = jnp.float32
BF16 = jnp.bfloat16

SETS = 8
ROWS = 16
SLOTS = 3
ORDERS = ((0, 1, 2, 3), (1, 0, 3, 2), (2, 3, 0, 1), (3, 2, 1, 0))


def dot(a, b):
    return jnp.dot(a, b, preferred_element_type=F32)


def dot_nt(a, b):
    return lax.dot_general(a, b, (((1,), (1,)), ((), ())), preferred_element_type=F32)


def iota(shape, dim):
    return lax.broadcasted_iota(jnp.int32, shape, dim)


def flip(value, bits):
    if bits == 1:
        return value + 1 - 2 * lax.rem(value, 2)
    if bits == 2:
        return 3 - value
    if bits == 3:
        return lax.rem(value + 2, 4)
    return value


def moved(local, bits):
    y, x = local // 4, lax.rem(local, 4)
    return flip(y, bits & 3) * 4 + flip(x, bits >> 2)


def one(mask):
    return jnp.where(mask, 1.0, 0.0).astype(BF16)


def kernel(
    groups,
    ids_ref, count_ref, gates_ref, tok_ref, gate_hbm, up_hbm, down_hbm,
    out_ref,
    w_in, w_down, acc, hid,
    take, give, meta_s, meta_r, meta_p, codes, sel, weigh, sel_tmp,
    w_sem, zm_send, zm_recv, pm_send, pm_recv,
    zd_send, zd_recv, zc_send, zc_recv,
    xd_send, xd_recv, xc_send, xc_recv,
    zs, zr, zb, r1, p1, g3, s2, f1,
):
    tokens = tok_ref.shape[0]
    width = hid.shape[1]
    held = groups * ROWS
    pad = groups * SLOTS
    segments = groups * 16
    cols = r1.shape[2]
    set_cols = 4 * cols
    g = lax.axis_index("group")
    l = lax.axis_index("local")

    def rows_of(index):
        return pl.ds(pl.multiple_of(index * ROWS, ROWS), ROWS)

    def columns(index, wide):
        return pl.ds(pl.multiple_of(index * wide, wide), wide)

    def peer(j):
        return lax.rem(g + j, groups)

    barrier = pltpu.get_barrier_semaphore()

    def loop(low, high, step):
        def body(n, carry):
            step(n)
            return carry

        lax.fori_loop(low, high, body, 0)

    loop(1, groups, lambda j: pl.semaphore_signal(barrier, inc=1, device_id=(peer(j), l), device_id_type=MESH))
    for e in range(4):
        pl.semaphore_signal(barrier, inc=1, device_id=(g, moved(l, 1 << e)), device_id_type=MESH)

    weights = [
        pltpu.make_async_copy(gate_hbm.at[0], w_in.at[:, 0:width], w_sem.at[0]),
        pltpu.make_async_copy(up_hbm.at[0], w_in.at[:, width : 2 * width], w_sem.at[1]),
        pltpu.make_async_copy(down_hbm.at[0], w_down, w_sem.at[2]),
    ]
    for copy in weights:
        copy.start()

    ids = jnp.where(iota(ids_ref.shape, 0) < count_ref[...], ids_ref[...], -1)
    gates = gates_ref[...].astype(F32)
    label = iota((segments, tokens), 0)
    seg_gate = jnp.zeros((segments, tokens), F32)
    for k in range(ids.shape[0]):
        seg_gate += jnp.where(ids[k : k + 1] == label, gates[k : k + 1], 0.0)
    is_named = seg_gate > 0
    named = one(is_named)
    in_group = one(iota((segments, 128), 0) // 16 == iota((segments, 128), 1))
    in_group_t = one(iota((128, segments), 0) == iota((128, segments), 1) // 16)
    earlier = one(iota((tokens, tokens), 0) < iota((tokens, tokens), 1))
    visit = dot(in_group_t, named) > 0
    place = jnp.where(visit, dot(one(visit), earlier), -1.0)
    take[...] = one(dot(in_group, place.astype(BF16)) == (iota((held, tokens), 0) % ROWS).astype(F32))
    rank = jnp.where(is_named, dot(named, earlier) + 1.0, 0.0).astype(BF16)
    own_group = iota((held, segments), 0) // ROWS == iota((held, segments), 1) // 16
    fold = one(iota((segments, 128), 0) % 16 == iota((segments, 128), 1))
    fold_far = one(iota((segments, 128), 0) % 16 + 16 == iota((segments, 128), 1))
    ranks = jnp.where(own_group, dot_nt(take[...], rank), 0.0).astype(BF16)
    row_gates = jnp.where(own_group, dot_nt(take[...], seg_gate.astype(BF16)), 0.0).astype(BF16)
    meta_s[...] = (dot(ranks, fold) + dot(row_gates, fold_far)).astype(BF16)

    def gather(k):
        zs[k] = dot(take[...], tok_ref[:, columns(k, set_cols)]).astype(BF16)

    loop(0, SETS, gather)
    acc[...] = jnp.zeros_like(acc)
    eye = one(iota((128, 128), 0) == iota((128, 128), 1))
    eye_held = one(iota((held, held), 0) == iota((held, held), 1))
    eye_tokens = one(iota((tokens, tokens), 0) == iota((tokens, tokens), 1))
    give[...] = dot_nt(eye_tokens, take[...]).astype(BF16)
    meta_r[rows_of(g), :] = meta_s[rows_of(g), :]
    for copy in weights:
        copy.wait()
    pl.semaphore_wait(barrier, groups - 1 + 4)

    def meta_copy(j):
        return pltpu.make_async_remote_copy(
            src_ref=meta_s.at[rows_of(peer(j))], dst_ref=meta_r.at[rows_of(g)],
            send_sem=zm_send, recv_sem=zm_recv,
            device_id=(peer(j), l), device_id_type=MESH,
        )

    def out_copy(k, j):
        return pltpu.make_async_remote_copy(
            src_ref=zs.at[k, rows_of(peer(j)), :], dst_ref=zr.at[k, rows_of(g), :],
            send_sem=zd_send.at[k], recv_sem=zd_recv.at[k],
            device_id=(peer(j), l), device_id_type=MESH,
        )

    def back_copy(k, j):
        return pltpu.make_async_remote_copy(
            src_ref=zr.at[k, rows_of(peer(j)), :], dst_ref=zb.at[k, rows_of(g), :],
            send_sem=zc_send.at[k], recv_sem=zc_recv.at[k],
            device_id=(peer(j), l), device_id_type=MESH,
        )

    def start_all(make):
        loop(1, groups, lambda j: make(j).start())

    def settle(like, send, recv):
        pltpu.make_async_remote_copy(
            src_ref=like, dst_ref=like, send_sem=send, recv_sem=recv,
            device_id=(peer(1), l), device_id_type=MESH,
        ).wait()

    others = held - ROWS

    def start_out(k):
        start_all(functools.partial(out_copy, k))

    def exchange(e, src, dst, send, recv):
        return pltpu.make_async_remote_copy(
            src_ref=src, dst_ref=dst, send_sem=send, recv_sem=recv,
            device_id=(g, moved(l, 1 << e)), device_id_type=MESH,
        )

    def forth(k, v, step):
        i = k * 4 + v
        src, dst = (
            (zr.at[k, :, v * cols : (v + 1) * cols], r1.at[i]),
            (s2.at[i], g3.at[i, 0:2, :, 1]),
            (g3.at[i, 0], g3.at[i, 2]),
            (g3.at[i, 1:3, 1], f1.at[i]),
        )[step]
        return exchange(ORDERS[v][step], src, dst, xd_send.at[step, k], xd_recv.at[step, k])

    def back(k, v, step):
        i = k * 4 + v
        src, dst = (
            (r1.at[i], p1.at[i]),
            (g3.at[i, 0:2, :, 1], s2.at[i]),
            (g3.at[i, 2], g3.at[i, 0]),
            (f1.at[i], g3.at[i, 1:3, 1]),
        )[step]
        return exchange(ORDERS[v][step], src, dst, xc_send.at[step, k], xc_recv.at[step, k])

    def four(k, step):
        return (r1 if step == 0 else s2).at[pl.ds(k * 4, 4)]

    def forth_wait(k, step):
        settle(four(k, step), xd_send.at[step, k], xd_recv.at[step, k])

    def back_wait(k, step):
        settle(four(k, step), xc_send.at[step, k], xc_recv.at[step, k])

    def partner_meta(e):
        return exchange(e, meta_r, meta_p.at[e], pm_send.at[e], pm_recv.at[e])

    start_all(meta_copy)
    start_out(0)
    start_out(1)
    settle(meta_r.at[0:others], zm_send, zm_recv)
    for e in range(4):
        partner_meta(e).start()

    first = (iota((16, held), 1) // ROWS * SLOTS - 1).astype(F32)
    slot = iota((pad, held), 0).astype(F32)

    def decode(index, meta):
        turned = dot_nt(eye, meta)
        codes[index, 0:16] = jnp.where(turned[0:16] > 0, first + turned[0:16], -1.0)
        codes[index, 16:32] = turned[16:32]

    def hits(v, r):
        e1, e2, e3, e4 = ORDERS[v]
        index = 1 + e1 if r else 0
        for b in range(8):
            d2, q, d4 = b >> 2, b >> 1 & 1, b & 1
            segment = moved(l, d2 << e2 | (1 - q) << e3 | d4 << e4)
            hit = slot == codes[index, pl.ds(segment, 1), :]
            yield slice(b * pad, (b + 1) * pad), hit, codes[index, pl.ds(segment + 16, 1), :]

    def build_sel(v, r):
        for at, hit, _ in hits(v, r):
            sel[v, r, at, :] = one(hit)

    def build_weigh(v, r):
        for at, hit, gate in hits(v, r):
            sel_tmp[at, :] = jnp.where(hit, gate, 0.0).astype(BF16)
        weigh[v, r] = dot_nt(eye_held, sel_tmp[...]).astype(BF16)

    decode(0, meta_r[...])
    for v in range(4):
        build_sel(v, 0)

    def partners():
        for e in range(4):
            partner_meta(e).wait()
            decode(1 + e, meta_p[e])
        for v in range(4):
            build_sel(v, 1)

    def select(k, v, r, rows):
        i = k * 4 + v
        chosen = dot(sel[v, r], rows).astype(BF16)
        inner = slice(r * pad, (r + 1) * pad)
        for b in range(4):
            q, d4 = b >> 1, b & 1
            s2[i, q, d4, inner, :] = chosen[(4 + b) * pad : (5 + b) * pad]
            g3[i, q, d4, 0, inner, :] = chosen[b * pad : (b + 1) * pad]

    def block_of(v, r4, b):
        e1, e2, e3, e4 = ORDERS[v]
        return r4 << e4 | (b >> 2) << e3 | (b >> 1 & 1) << e2 | (b & 1) << e1

    def accumulate(k, v, r4, rows):
        part = dot(rows.reshape(8 * pad, cols), w_in[columns(k * 4 + v, cols), :])
        for b in range(8):
            acc[block_of(v, r4, b)] += part[b * pad : (b + 1) * pad]

    def forth_0(k):
        zr[k, rows_of(g), :] = zs[k, rows_of(g), :]
        settle(zr.at[k, 0:others], zd_send.at[k], zd_recv.at[k])
        for v in range(4):
            forth(k, v, 0).start()

        @pl.when(k + 2 < SETS)
        def _():
            start_out(k + 2)

    def forth_own(k):
        for v in range(4):
            select(k, v, 0, zr[k, :, v * cols : (v + 1) * cols])

    def forth_1(k):
        forth_wait(k, 0)
        for v in range(4):
            select(k, v, 1, r1[k * 4 + v])
            forth(k, v, 1).start()

    def forth_2(k):
        forth_wait(k, 1)
        for v in range(4):
            forth(k, v, 2).start()

    def forth_3(k):
        forth_wait(k, 2)
        for v in range(4):
            forth(k, v, 3).start()

    def forth_near(k):
        for v in range(4):
            accumulate(k, v, 0, g3[k * 4 + v, 1:3, 0])

    def forth_far(k):
        forth_wait(k, 3)
        for v in range(4):
            accumulate(k, v, 1, f1[k * 4 + v])

    def back_3(k):
        for v in range(4):
            i = k * 4 + v
            result = dot(hid[...], w_down[:, columns(i, cols)]).astype(BF16)
            for r4 in (1, 0):
                for b in range(8):
                    r3, r2, r1_ = b >> 2, b >> 1 & 1, b & 1
                    inner = slice(r1_ * pad, (r1_ + 1) * pad)
                    c = block_of(v, r4, b)
                    if r4:
                        f1[i, r3, r2, inner, :] = result[c * pad : (c + 1) * pad]
                    else:
                        g3[i, 1 + r3, 0, r2, inner, :] = result[c * pad : (c + 1) * pad]
                if r4:
                    back(k, v, 3).start()

    def back_2(k):
        back_wait(k, 3)
        for v in range(4):
            back(k, v, 2).start()

    def back_1(k):
        back_wait(k, 2)
        for v in range(4):
            back(k, v, 1).start()

    def part_sum(k, v, r):
        i = k * 4 + v
        inner = slice(r * pad, (r + 1) * pad)
        near = g3[i, 0:2, :, 0, inner, :].reshape(4 * pad, cols)
        far = s2[i, :, :, inner, :].reshape(4 * pad, cols)
        return dot(weigh[v, r], jnp.concatenate([near, far], axis=0))

    def back_0(k):
        back_wait(k, 1)
        for v in range(4):
            r1[k * 4 + v] = part_sum(k, v, 1).astype(BF16)
            back(k, v, 0).start()

    def back_own(k):
        back_wait(k, 0)
        for v in range(4):
            own = part_sum(k, v, 0)
            zr[k, :, v * cols : (v + 1) * cols] = (own + p1[k * 4 + v].astype(F32)).astype(BF16)
        start_all(functools.partial(back_copy, k))
        zb[k, rows_of(g), :] = zr[k, rows_of(g), :]

    def back_out(k):
        settle(zb.at[k, 0:others], zc_send.at[k], zc_recv.at[k])
        out_ref[:, columns(k, set_cols)] = dot(give[...], zb[k]).astype(BF16)

    def staggered(stages, once):
        depth = 1 + max(lag for lag, _ in stages)

        def slot_step(t):
            for lag, stage in stages:
                k = t - lag

                @pl.when((k >= 0) & (k < SETS))
                def _(stage=stage, k=k):
                    stage(k)

            for at, extra in once:
                pl.when(t == at)(extra)

        loop(0, SETS + depth - 1, slot_step)

    def weights_back():
        for v in range(4):
            for r in range(2):
                build_weigh(v, r)

    staggered(
        ((4, forth_far), (3, forth_3), (2, forth_2), (1, forth_1), (0, forth_0), (0, forth_own), (3, forth_near)),
        ((0, partners), (3, weights_back)),
    )
    for c in range(16):
        gated = acc[c, :, 0:width]
        upward = acc[c, :, width : 2 * width]
        hid[c * pad : (c + 1) * pad, :] = (gated / (1.0 + jnp.exp(-gated)) * upward).astype(BF16)
    staggered(((0, back_3), (1, back_2), (2, back_1), (3, back_0), (4, back_own), (6, back_out)), ())


def on_device(tokens, segment_ids, segment_count, gate_values, gate_weight, up_weight, down_weight):
    groups = lax.axis_size("group")
    model = tokens.shape[1]
    width = gate_weight.shape[2]
    held = groups * ROWS
    pad = groups * SLOTS
    cols = model // (4 * SETS)
    vmem = pl.BlockSpec(memory_space=pltpu.VMEM)
    hbm = pl.BlockSpec(memory_space=pl.ANY)
    dma = pltpu.SemaphoreType.DMA

    def per_set():
        return pltpu.VMEM((SETS, held, 4 * cols), BF16)

    def per_item(*shape):
        return pltpu.VMEM((SETS * 4,) + shape + (cols,), BF16)

    return pl.pallas_call(
        functools.partial(kernel, groups),
        out_shape=jax.ShapeDtypeStruct(tokens.shape, BF16),
        in_specs=[vmem, vmem, vmem, vmem, hbm, hbm, hbm],
        out_specs=vmem,
        scratch_shapes=[
            pltpu.VMEM((model, 2 * width), BF16),
            pltpu.VMEM((width, model), BF16),
            pltpu.VMEM((16, pad, 2 * width), F32),
            pltpu.VMEM((16 * pad, width), BF16),
            pltpu.VMEM((held, tokens.shape[0]), BF16),
            pltpu.VMEM((tokens.shape[0], held), BF16),
            pltpu.VMEM((held, 128), BF16),
            pltpu.VMEM((held, 128), BF16),
            pltpu.VMEM((4, held, 128), BF16),
            pltpu.VMEM((5, 32, held), F32),
            pltpu.VMEM((4, 2, 8 * pad, held), BF16),
            pltpu.VMEM((4, 2, held, 8 * pad), BF16),
            pltpu.VMEM((8 * pad, held), BF16),
            dma((3,)),
            dma, dma, dma((4,)), dma((4,)),
            *[dma((SETS,))] * 4,
            *[dma((4, SETS))] * 4,
            per_set(), per_set(), per_set(),
            per_item(held), per_item(held),
            per_item(3, 2, 2, 2 * pad),
            per_item(2, 2, 2 * pad), per_item(2, 2, 2 * pad),
        ],
        compiler_params=pltpu.CompilerParams(
            collective_id=0, has_side_effects=True, vmem_limit_bytes=56 * 1024 * 1024
        ),
    )(segment_ids.T, segment_count[None, :], gate_values.T, tokens, gate_weight, up_weight, down_weight)


def solution(mesh):
    return jax.shard_map(
        on_device,
        mesh=mesh,
        in_specs=(
            P(("group", "local"), None),
            P(("group", "local"), None),
            P(("group", "local")),
            P(("group", "local"), None),
            P(("group", "local"), None, None),
            P(("group", "local"), None, None),
            P(("group", "local"), None, None),
        ),
        out_specs=P(("group", "local"), None),
        check_vma=False,
    )
```

```python
import functools

import jax
import jax.numpy as jnp
from jax import lax
from jax.experimental import pallas as pl
from jax.experimental.pallas import tpu as pltpu
from jax.sharding import PartitionSpec as P

MESH = pl.DeviceIdType.MESH
F32 = jnp.float32
BF16 = jnp.bfloat16

SETS = 8
ROWS = 16
SLOTS = 3
ORDERS = ((0, 1, 2, 3), (1, 0, 3, 2), (2, 3, 0, 1), (3, 2, 1, 0))


def dot(a, b):
    return jnp.dot(a, b, preferred_element_type=F32)


def dot_nt(a, b):
    return lax.dot_general(a, b, (((1,), (1,)), ((), ())), preferred_element_type=F32)


def iota(shape, dim):
    return lax.broadcasted_iota(jnp.int32, shape, dim)


def flip(value, bits):
    if bits == 1:
        return value + 1 - 2 * lax.rem(value, 2)
    if bits == 2:
        return 3 - value
    if bits == 3:
        return lax.rem(value + 2, 4)
    return value


def moved(local, bits):
    y, x = local // 4, lax.rem(local, 4)
    return flip(y, bits & 3) * 4 + flip(x, bits >> 2)


def one(mask):
    return jnp.where(mask, 1.0, 0.0).astype(BF16)


def kernel(
    groups,
    ids_ref, count_ref, gates_ref, tok_ref, gate_hbm, up_hbm, down_hbm,
    out_ref,
    w_in, w_down, acc, hid,
    take, give, meta_s, meta_r, meta_p, codes, sel, weigh, sel_tmp,
    w_sem, zm_send, zm_recv, pm_send, pm_recv,
    zd_send, zd_recv, zc_send, zc_recv,
    xd_send, xd_recv, xc_send, xc_recv,
    zs, zr, zb, r1, p1, g3, s2, f1,
):
    tokens = tok_ref.shape[0]
    width = hid.shape[1]
    held = groups * ROWS
    pad = groups * SLOTS
    segments = groups * 16
    cols = r1.shape[2]
    set_cols = 4 * cols
    g = lax.axis_index("group")
    l = lax.axis_index("local")

    def rows_of(index):
        return pl.ds(pl.multiple_of(index * ROWS, ROWS), ROWS)

    def columns(index, wide):
        return pl.ds(pl.multiple_of(index * wide, wide), wide)

    def peer(j):
        return lax.rem(g + j, groups)

    barrier = pltpu.get_barrier_semaphore()

    def loop(low, high, step):
        def body(n, carry):
            step(n)
            return carry

        lax.fori_loop(low, high, body, 0)

    loop(1, groups, lambda j: pl.semaphore_signal(barrier, inc=1, device_id=(peer(j), l), device_id_type=MESH))
    for e in range(4):
        pl.semaphore_signal(barrier, inc=1, device_id=(g, moved(l, 1 << e)), device_id_type=MESH)

    weights = [
        pltpu.make_async_copy(gate_hbm.at[0], w_in.at[:, 0:width], w_sem.at[0]),
        pltpu.make_async_copy(up_hbm.at[0], w_in.at[:, width : 2 * width], w_sem.at[1]),
        pltpu.make_async_copy(down_hbm.at[0], w_down, w_sem.at[2]),
    ]
    for copy in weights:
        copy.start()

    ids = jnp.where(iota(ids_ref.shape, 0) < count_ref[...], ids_ref[...], -1)
    gates = gates_ref[...].astype(F32)
    label = iota((segments, tokens), 0)
    seg_gate = jnp.zeros((segments, tokens), F32)
    for k in range(ids.shape[0]):
        seg_gate += jnp.where(ids[k : k + 1] == label, gates[k : k + 1], 0.0)
    is_named = seg_gate > 0
    named = one(is_named)
    in_group = one(iota((segments, 128), 0) // 16 == iota((segments, 128), 1))
    in_group_t = one(iota((128, segments), 0) == iota((128, segments), 1) // 16)
    earlier = one(iota((tokens, tokens), 0) < iota((tokens, tokens), 1))
    visit = dot(in_group_t, named) > 0
    place = jnp.where(visit, dot(one(visit), earlier), -1.0)
    take[...] = one(dot(in_group, place.astype(BF16)) == (iota((held, tokens), 0) % ROWS).astype(F32))
    rank = jnp.where(is_named, dot(named, earlier) + 1.0, 0.0).astype(BF16)
    own_group = iota((held, segments), 0) // ROWS == iota((held, segments), 1) // 16
    fold = one(iota((segments, 128), 0) % 16 == iota((segments, 128), 1))
    fold_far = one(iota((segments, 128), 0) % 16 + 16 == iota((segments, 128), 1))
    ranks = jnp.where(own_group, dot_nt(take[...], rank), 0.0).astype(BF16)
    row_gates = jnp.where(own_group, dot_nt(take[...], seg_gate.astype(BF16)), 0.0).astype(BF16)
    meta_s[...] = (dot(ranks, fold) + dot(row_gates, fold_far)).astype(BF16)

    def gather(k):
        zs[k] = dot(take[...], tok_ref[:, columns(k, set_cols)]).astype(BF16)

    loop(0, SETS, gather)
    acc[...] = jnp.zeros_like(acc)
    eye = one(iota((128, 128), 0) == iota((128, 128), 1))
    eye_held = one(iota((held, held), 0) == iota((held, held), 1))
    eye_tokens = one(iota((tokens, tokens), 0) == iota((tokens, tokens), 1))
    give[...] = dot_nt(eye_tokens, take[...]).astype(BF16)
    meta_r[rows_of(g), :] = meta_s[rows_of(g), :]
    for copy in weights:
        copy.wait()
    pl.semaphore_wait(barrier, groups - 1 + 4)

    def meta_copy(j):
        return pltpu.make_async_remote_copy(
            src_ref=meta_s.at[rows_of(peer(j))], dst_ref=meta_r.at[rows_of(g)],
            send_sem=zm_send, recv_sem=zm_recv,
            device_id=(peer(j), l), device_id_type=MESH,
        )

    def out_copy(k, j):
        return pltpu.make_async_remote_copy(
            src_ref=zs.at[k, rows_of(peer(j)), :], dst_ref=zr.at[k, rows_of(g), :],
            send_sem=zd_send.at[k], recv_sem=zd_recv.at[k],
            device_id=(peer(j), l), device_id_type=MESH,
        )

    def back_copy(k, n, j):
        return pltpu.make_async_remote_copy(
            src_ref=zr.at[pl.ds(k, n), rows_of(peer(j)), :], dst_ref=zb.at[pl.ds(k, n), rows_of(g), :],
            send_sem=zc_send.at[k], recv_sem=zc_recv.at[k],
            device_id=(peer(j), l), device_id_type=MESH,
        )

    def start_all(make):
        loop(1, groups, lambda j: make(j).start())

    def settle(like, send, recv):
        pltpu.make_async_remote_copy(
            src_ref=like, dst_ref=like, send_sem=send, recv_sem=recv,
            device_id=(peer(1), l), device_id_type=MESH,
        ).wait()

    others = held - ROWS

    def start_out(k):
        start_all(functools.partial(out_copy, k))

    def exchange(e, src, dst, send, recv):
        return pltpu.make_async_remote_copy(
            src_ref=src, dst_ref=dst, send_sem=send, recv_sem=recv,
            device_id=(g, moved(l, 1 << e)), device_id_type=MESH,
        )

    def forth(k, v, step):
        i = k * 4 + v
        src, dst = (
            (zr.at[k, :, v * cols : (v + 1) * cols], r1.at[i]),
            (s2.at[i], g3.at[i, 0:2, :, 1]),
            (g3.at[i, 0], g3.at[i, 2]),
            (g3.at[i, 1:3, 1], f1.at[i]),
        )[step]
        return exchange(ORDERS[v][step], src, dst, xd_send.at[step, k], xd_recv.at[step, k])

    def back(k, v, step):
        i = k * 4 + v
        src, dst = (
            (r1.at[i], p1.at[i]),
            (g3.at[i, 0:2, :, 1], s2.at[i]),
            (g3.at[i, 2], g3.at[i, 0]),
            (f1.at[i], g3.at[i, 1:3, 1]),
        )[step]
        return exchange(ORDERS[v][step], src, dst, xc_send.at[step, k], xc_recv.at[step, k])

    def four(k, step):
        return (r1 if step == 0 else s2).at[pl.ds(k * 4, 4)]

    def forth_wait(k, step):
        settle(four(k, step), xd_send.at[step, k], xd_recv.at[step, k])

    def back_wait(k, step):
        settle(four(k, step), xc_send.at[step, k], xc_recv.at[step, k])

    def partner_meta(e):
        return exchange(e, meta_r, meta_p.at[e], pm_send.at[e], pm_recv.at[e])

    start_all(meta_copy)
    start_out(0)
    start_out(1)
    settle(meta_r.at[0:others], zm_send, zm_recv)
    for e in range(4):
        partner_meta(e).start()

    first = (iota((16, held), 1) // ROWS * SLOTS - 1).astype(F32)
    slot = iota((pad, held), 0).astype(F32)

    def decode(index, meta):
        turned = dot_nt(eye, meta)
        codes[index, 0:16] = jnp.where(turned[0:16] > 0, first + turned[0:16], -1.0)
        codes[index, 16:32] = turned[16:32]

    def hits(v, r):
        e1, e2, e3, e4 = ORDERS[v]
        index = 1 + e1 if r else 0
        for b in range(8):
            d2, q, d4 = b >> 2, b >> 1 & 1, b & 1
            segment = moved(l, d2 << e2 | (1 - q) << e3 | d4 << e4)
            hit = slot == codes[index, pl.ds(segment, 1), :]
            yield slice(b * pad, (b + 1) * pad), hit, codes[index, pl.ds(segment + 16, 1), :]

    def build_sel(v, r):
        for at, hit, _ in hits(v, r):
            sel[v, r, at, :] = one(hit)

    def build_weigh(v, r):
        for at, hit, gate in hits(v, r):
            sel_tmp[at, :] = jnp.where(hit, gate, 0.0).astype(BF16)
        weigh[v, r] = dot_nt(eye_held, sel_tmp[...]).astype(BF16)

    decode(0, meta_r[...])
    for v in range(4):
        build_sel(v, 0)

    def partners():
        for e in range(4):
            partner_meta(e).wait()
            decode(1 + e, meta_p[e])
        for v in range(4):
            build_sel(v, 1)

    def select(k, v, r, rows):
        i = k * 4 + v
        chosen = dot(sel[v, r], rows).astype(BF16)
        inner = slice(r * pad, (r + 1) * pad)
        for b in range(4):
            q, d4 = b >> 1, b & 1
            s2[i, q, d4, inner, :] = chosen[(4 + b) * pad : (5 + b) * pad]
            g3[i, q, d4, 0, inner, :] = chosen[b * pad : (b + 1) * pad]

    def block_of(v, r4, b):
        e1, e2, e3, e4 = ORDERS[v]
        return r4 << e4 | (b >> 2) << e3 | (b >> 1 & 1) << e2 | (b & 1) << e1

    def accumulate(k, v, r4, rows):
        part = dot(rows.reshape(8 * pad, cols), w_in[columns(k * 4 + v, cols), :])
        for b in range(8):
            acc[block_of(v, r4, b)] += part[b * pad : (b + 1) * pad]

    def forth_0(k):
        zr[k, rows_of(g), :] = zs[k, rows_of(g), :]
        settle(zr.at[k, 0:others], zd_send.at[k], zd_recv.at[k])
        for v in range(4):
            forth(k, v, 0).start()

        @pl.when(k + 2 < SETS)
        def _():
            start_out(k + 2)

    def forth_own(k):
        for v in range(4):
            select(k, v, 0, zr[k, :, v * cols : (v + 1) * cols])

    def forth_1(k):
        forth_wait(k, 0)
        for v in range(4):
            select(k, v, 1, r1[k * 4 + v])
            forth(k, v, 1).start()

    def forth_2(k):
        forth_wait(k, 1)
        for v in range(4):
            forth(k, v, 2).start()

    def forth_3(k):
        forth_wait(k, 2)
        for v in range(4):
            forth(k, v, 3).start()

    def forth_near(k):
        for v in range(4):
            accumulate(k, v, 0, g3[k * 4 + v, 1:3, 0])

    def forth_far(k):
        forth_wait(k, 3)
        for v in range(4):
            accumulate(k, v, 1, f1[k * 4 + v])

    def back_3(k):
        for v in range(4):
            i = k * 4 + v
            result = dot(hid[...], w_down[:, columns(i, cols)]).astype(BF16)
            for r4 in (1, 0):
                for b in range(8):
                    r3, r2, r1_ = b >> 2, b >> 1 & 1, b & 1
                    inner = slice(r1_ * pad, (r1_ + 1) * pad)
                    c = block_of(v, r4, b)
                    if r4:
                        f1[i, r3, r2, inner, :] = result[c * pad : (c + 1) * pad]
                    else:
                        g3[i, 1 + r3, 0, r2, inner, :] = result[c * pad : (c + 1) * pad]
                if r4:
                    back(k, v, 3).start()

    def back_2(k):
        back_wait(k, 3)
        for v in range(4):
            back(k, v, 2).start()

    def back_1(k):
        back_wait(k, 2)
        for v in range(4):
            back(k, v, 1).start()

    def part_sum(k, v, r):
        i = k * 4 + v
        inner = slice(r * pad, (r + 1) * pad)
        near = g3[i, 0:2, :, 0, inner, :].reshape(4 * pad, cols)
        far = s2[i, :, :, inner, :].reshape(4 * pad, cols)
        return dot(weigh[v, r], jnp.concatenate([near, far], axis=0))

    def back_0(k):
        back_wait(k, 1)
        for v in range(4):
            r1[k * 4 + v] = part_sum(k, v, 1).astype(BF16)
            back(k, v, 0).start()

    def back_own(k):
        back_wait(k, 0)
        for v in range(4):
            own = part_sum(k, v, 0)
            zr[k, :, v * cols : (v + 1) * cols] = (own + p1[k * 4 + v].astype(F32)).astype(BF16)
        zb[k, rows_of(g), :] = zr[k, rows_of(g), :]
        paired(k, lambda first, n: start_all(functools.partial(back_copy, first, n)))

    def paired(k, step):
        pl.when(k >= SETS - 2)(lambda: step(k, 1))
        pl.when((k < SETS - 2) & (lax.rem(k, 2) == 1))(lambda: step(k - 1, 2))

    def back_out(k):
        def take_in(first, n):
            settle(zb.at[pl.ds(first, n), 0:others], zc_send.at[first], zc_recv.at[first])
            for m in range(n):
                out_ref[:, columns(first + m, set_cols)] = dot(give[...], zb[first + m]).astype(BF16)

        paired(k, take_in)

    def staggered(stages, once):
        depth = 1 + max(lag for lag, _ in stages)

        def slot_step(t):
            for lag, stage in stages:
                k = t - lag

                @pl.when((k >= 0) & (k < SETS))
                def _(stage=stage, k=k):
                    stage(k)

            for at, extra in once:
                pl.when(t == at)(extra)

        loop(0, SETS + depth - 1, slot_step)

    def weights_back():
        for v in range(4):
            for r in range(2):
                build_weigh(v, r)

    staggered(
        ((4, forth_far), (3, forth_3), (2, forth_2), (1, forth_1), (0, forth_0), (0, forth_own), (3, forth_near)),
        ((0, partners), (3, weights_back)),
    )
    for c in range(16):
        gated = acc[c, :, 0:width]
        upward = acc[c, :, width : 2 * width]
        hid[c * pad : (c + 1) * pad, :] = (gated / (1.0 + jnp.exp(-gated)) * upward).astype(BF16)
    staggered(((0, back_3), (1, back_2), (2, back_1), (3, back_0), (4, back_own), (6, back_out)), ())


def on_device(tokens, segment_ids, segment_count, gate_values, gate_weight, up_weight, down_weight):
    groups = lax.axis_size("group")
    model = tokens.shape[1]
    width = gate_weight.shape[2]
    held = groups * ROWS
    pad = groups * SLOTS
    cols = model // (4 * SETS)
    vmem = pl.BlockSpec(memory_space=pltpu.VMEM)
    hbm = pl.BlockSpec(memory_space=pl.ANY)
    dma = pltpu.SemaphoreType.DMA

    def per_set():
        return pltpu.VMEM((SETS, held, 4 * cols), BF16)

    def per_item(*shape):
        return pltpu.VMEM((SETS * 4,) + shape + (cols,), BF16)

    return pl.pallas_call(
        functools.partial(kernel, groups),
        out_shape=jax.ShapeDtypeStruct(tokens.shape, BF16),
        in_specs=[vmem, vmem, vmem, vmem, hbm, hbm, hbm],
        out_specs=vmem,
        scratch_shapes=[
            pltpu.VMEM((model, 2 * width), BF16),
            pltpu.VMEM((width, model), BF16),
            pltpu.VMEM((16, pad, 2 * width), F32),
            pltpu.VMEM((16 * pad, width), BF16),
            pltpu.VMEM((held, tokens.shape[0]), BF16),
            pltpu.VMEM((tokens.shape[0], held), BF16),
            pltpu.VMEM((held, 128), BF16),
            pltpu.VMEM((held, 128), BF16),
            pltpu.VMEM((4, held, 128), BF16),
            pltpu.VMEM((5, 32, held), F32),
            pltpu.VMEM((4, 2, 8 * pad, held), BF16),
            pltpu.VMEM((4, 2, held, 8 * pad), BF16),
            pltpu.VMEM((8 * pad, held), BF16),
            dma((3,)),
            dma, dma, dma((4,)), dma((4,)),
            *[dma((SETS,))] * 4,
            *[dma((4, SETS))] * 4,
            per_set(), per_set(), per_set(),
            per_item(held), per_item(held),
            per_item(3, 2, 2, 2 * pad),
            per_item(2, 2, 2 * pad), per_item(2, 2, 2 * pad),
        ],
        compiler_params=pltpu.CompilerParams(
            collective_id=0, has_side_effects=True, vmem_limit_bytes=56 * 1024 * 1024
        ),
    )(segment_ids.T, segment_count[None, :], gate_values.T, tokens, gate_weight, up_weight, down_weight)


def solution(mesh):
    return jax.shard_map(
        on_device,
        mesh=mesh,
        in_specs=(
            P(("group", "local"), None),
            P(("group", "local"), None),
            P(("group", "local")),
            P(("group", "local"), None),
            P(("group", "local"), None, None),
            P(("group", "local"), None, None),
            P(("group", "local"), None, None),
        ),
        out_specs=P(("group", "local"), None),
        check_vma=False,
    )
```

```python
import functools

import jax
import jax.numpy as jnp
from jax import lax
from jax.experimental import pallas as pl
from jax.experimental.pallas import tpu as pltpu
from jax.sharding import PartitionSpec as P

MESH = pl.DeviceIdType.MESH
F32 = jnp.float32
BF16 = jnp.bfloat16

SETS = 8
ROWS = 16
SLOTS = 3
ORDERS = ((0, 1, 2, 3), (1, 0, 3, 2), (2, 3, 0, 1), (3, 2, 1, 0))


def dot(a, b):
    return jnp.dot(a, b, preferred_element_type=F32)


def dot_nt(a, b):
    return lax.dot_general(a, b, (((1,), (1,)), ((), ())), preferred_element_type=F32)


def iota(shape, dim):
    return lax.broadcasted_iota(jnp.int32, shape, dim)


def flip(value, bits):
    if bits == 1:
        return value + 1 - 2 * lax.rem(value, 2)
    if bits == 2:
        return 3 - value
    if bits == 3:
        return lax.rem(value + 2, 4)
    return value


def moved(local, bits):
    y, x = local // 4, lax.rem(local, 4)
    return flip(y, bits & 3) * 4 + flip(x, bits >> 2)


def one(mask):
    return jnp.where(mask, 1.0, 0.0).astype(BF16)


def kernel(
    groups,
    ids_ref, count_ref, gates_ref, tok_ref, gate_hbm, up_hbm, down_hbm,
    out_ref,
    w_in, w_down, acc, hid,
    take, give, meta_s, meta_r, meta_p, codes, sel, weigh, sel_tmp,
    w_sem, zm_send, zm_recv, pm_send, pm_recv,
    zd_send, zd_recv, zc_send, zc_recv,
    xd_send, xd_recv, xc_send, xc_recv,
    zs, zr, zb, r1, p1, g3, s2, f1,
):
    tokens = tok_ref.shape[0]
    width = hid.shape[1]
    held = groups * ROWS
    pad = groups * SLOTS
    segments = groups * 16
    cols = r1.shape[2]
    set_cols = 4 * cols
    g = lax.axis_index("group")
    l = lax.axis_index("local")

    def rows_of(index):
        return pl.ds(pl.multiple_of(index * ROWS, ROWS), ROWS)

    def columns(index, wide):
        return pl.ds(pl.multiple_of(index * wide, wide), wide)

    def peer(j):
        return lax.rem(g + j, groups)

    barrier = pltpu.get_barrier_semaphore()

    def loop(low, high, step):
        def body(n, carry):
            step(n)
            return carry

        lax.fori_loop(low, high, body, 0)

    loop(1, groups, lambda j: pl.semaphore_signal(barrier, inc=1, device_id=(peer(j), l), device_id_type=MESH))
    for e in range(4):
        pl.semaphore_signal(barrier, inc=1, device_id=(g, moved(l, 1 << e)), device_id_type=MESH)

    weights = [
        pltpu.make_async_copy(gate_hbm.at[0], w_in.at[:, 0:width], w_sem.at[0]),
        pltpu.make_async_copy(up_hbm.at[0], w_in.at[:, width : 2 * width], w_sem.at[1]),
        pltpu.make_async_copy(down_hbm.at[0], w_down, w_sem.at[2]),
    ]
    for copy in weights:
        copy.start()

    ids = jnp.where(iota(ids_ref.shape, 0) < count_ref[...], ids_ref[...], -1)
    gates = gates_ref[...].astype(F32)
    label = iota((segments, tokens), 0)
    seg_gate = jnp.zeros((segments, tokens), F32)
    for k in range(ids.shape[0]):
        seg_gate += jnp.where(ids[k : k + 1] == label, gates[k : k + 1], 0.0)
    is_named = seg_gate > 0
    named = one(is_named)
    in_group = one(iota((segments, 128), 0) // 16 == iota((segments, 128), 1))
    in_group_t = one(iota((128, segments), 0) == iota((128, segments), 1) // 16)
    earlier = one(iota((tokens, tokens), 0) < iota((tokens, tokens), 1))
    visit = dot(in_group_t, named) > 0
    place = jnp.where(visit, dot(one(visit), earlier), -1.0)
    take[...] = one(dot(in_group, place.astype(BF16)) == (iota((held, tokens), 0) % ROWS).astype(F32))
    rank = jnp.where(is_named, dot(named, earlier) + 1.0, 0.0).astype(BF16)
    own_group = iota((held, segments), 0) // ROWS == iota((held, segments), 1) // 16
    fold = one(iota((segments, 128), 0) % 16 == iota((segments, 128), 1))
    fold_far = one(iota((segments, 128), 0) % 16 + 16 == iota((segments, 128), 1))
    ranks = jnp.where(own_group, dot_nt(take[...], rank), 0.0).astype(BF16)
    row_gates = jnp.where(own_group, dot_nt(take[...], seg_gate.astype(BF16)), 0.0).astype(BF16)
    meta_s[...] = (dot(ranks, fold) + dot(row_gates, fold_far)).astype(BF16)

    def gather(k):
        zs[k] = dot(take[...], tok_ref[:, columns(k, set_cols)]).astype(BF16)

    gather(0)
    gather(1)
    pl.semaphore_wait(barrier, groups - 1 + 4)

    def meta_copy(j):
        return pltpu.make_async_remote_copy(
            src_ref=meta_s.at[rows_of(peer(j))], dst_ref=meta_r.at[rows_of(g)],
            send_sem=zm_send, recv_sem=zm_recv,
            device_id=(peer(j), l), device_id_type=MESH,
        )

    def out_copy(k, j):
        return pltpu.make_async_remote_copy(
            src_ref=zs.at[k, rows_of(peer(j)), :], dst_ref=zr.at[k, rows_of(g), :],
            send_sem=zd_send.at[k], recv_sem=zd_recv.at[k],
            device_id=(peer(j), l), device_id_type=MESH,
        )

    def back_copy(k, j):
        return pltpu.make_async_remote_copy(
            src_ref=zr.at[k, rows_of(peer(j)), :], dst_ref=zb.at[k, rows_of(g), :],
            send_sem=zc_send.at[k], recv_sem=zc_recv.at[k],
            device_id=(peer(j), l), device_id_type=MESH,
        )

    def start_all(make):
        loop(1, groups, lambda j: make(j).start())

    def settle(like, send, recv):
        pltpu.make_async_remote_copy(
            src_ref=like, dst_ref=like, send_sem=send, recv_sem=recv,
            device_id=(peer(1), l), device_id_type=MESH,
        ).wait()

    others = held - ROWS

    def start_out(k):
        start_all(functools.partial(out_copy, k))

    def exchange(e, src, dst, send, recv):
        return pltpu.make_async_remote_copy(
            src_ref=src, dst_ref=dst, send_sem=send, recv_sem=recv,
            device_id=(g, moved(l, 1 << e)), device_id_type=MESH,
        )

    def forth(k, v, step):
        i = k * 4 + v
        src, dst = (
            (zr.at[k, :, v * cols : (v + 1) * cols], r1.at[i]),
            (s2.at[i], g3.at[i, 0:2, :, 1]),
            (g3.at[i, 0], g3.at[i, 2]),
            (g3.at[i, 1:3, 1], f1.at[i]),
        )[step]
        return exchange(ORDERS[v][step], src, dst, xd_send.at[step, k], xd_recv.at[step, k])

    def back(k, v, step):
        i = k * 4 + v
        src, dst = (
            (r1.at[i], p1.at[i]),
            (g3.at[i, 0:2, :, 1], s2.at[i]),
            (g3.at[i, 2], g3.at[i, 0]),
            (f1.at[i], g3.at[i, 1:3, 1]),
        )[step]
        return exchange(ORDERS[v][step], src, dst, xc_send.at[step, k], xc_recv.at[step, k])

    def four(k, step):
        return (r1 if step == 0 else s2).at[pl.ds(k * 4, 4)]

    def forth_wait(k, step):
        settle(four(k, step), xd_send.at[step, k], xd_recv.at[step, k])

    def back_wait(k, step):
        settle(four(k, step), xc_send.at[step, k], xc_recv.at[step, k])

    def partner_meta(e):
        return exchange(e, meta_r, meta_p.at[e], pm_send.at[e], pm_recv.at[e])

    start_all(meta_copy)
    start_out(0)
    start_out(1)
    loop(2, SETS, gather)
    acc[...] = jnp.zeros_like(acc)
    eye = one(iota((128, 128), 0) == iota((128, 128), 1))
    eye_held = one(iota((held, held), 0) == iota((held, held), 1))
    eye_tokens = one(iota((tokens, tokens), 0) == iota((tokens, tokens), 1))
    give[...] = dot_nt(eye_tokens, take[...]).astype(BF16)
    meta_r[rows_of(g), :] = meta_s[rows_of(g), :]
    settle(meta_r.at[0:others], zm_send, zm_recv)
    for e in range(4):
        partner_meta(e).start()

    first = (iota((16, held), 1) // ROWS * SLOTS - 1).astype(F32)
    slot = iota((pad, held), 0).astype(F32)

    def decode(index, meta):
        turned = dot_nt(eye, meta)
        codes[index, 0:16] = jnp.where(turned[0:16] > 0, first + turned[0:16], -1.0)
        codes[index, 16:32] = turned[16:32]

    def hits(v, r):
        e1, e2, e3, e4 = ORDERS[v]
        index = 1 + e1 if r else 0
        for b in range(8):
            d2, q, d4 = b >> 2, b >> 1 & 1, b & 1
            segment = moved(l, d2 << e2 | (1 - q) << e3 | d4 << e4)
            hit = slot == codes[index, pl.ds(segment, 1), :]
            yield slice(b * pad, (b + 1) * pad), hit, codes[index, pl.ds(segment + 16, 1), :]

    def build_sel(v, r):
        for at, hit, _ in hits(v, r):
            sel[v, r, at, :] = one(hit)

    def build_weigh(v, r):
        for at, hit, gate in hits(v, r):
            sel_tmp[at, :] = jnp.where(hit, gate, 0.0).astype(BF16)
        weigh[v, r] = dot_nt(eye_held, sel_tmp[...]).astype(BF16)

    decode(0, meta_r[...])
    for v in range(4):
        build_sel(v, 0)

    def partners():
        for e in range(4):
            partner_meta(e).wait()
            decode(1 + e, meta_p[e])
        for v in range(4):
            build_sel(v, 1)

    def select(k, v, r, rows):
        i = k * 4 + v
        chosen = dot(sel[v, r], rows).astype(BF16)
        inner = slice(r * pad, (r + 1) * pad)
        for b in range(4):
            q, d4 = b >> 1, b & 1
            s2[i, q, d4, inner, :] = chosen[(4 + b) * pad : (5 + b) * pad]
            g3[i, q, d4, 0, inner, :] = chosen[b * pad : (b + 1) * pad]

    def block_of(v, r4, b):
        e1, e2, e3, e4 = ORDERS[v]
        return r4 << e4 | (b >> 2) << e3 | (b >> 1 & 1) << e2 | (b & 1) << e1

    def accumulate(k, v, r4, rows):
        part = dot(rows.reshape(8 * pad, cols), w_in[columns(k * 4 + v, cols), :])
        for b in range(8):
            acc[block_of(v, r4, b)] += part[b * pad : (b + 1) * pad]

    def forth_0(k):
        zr[k, rows_of(g), :] = zs[k, rows_of(g), :]
        settle(zr.at[k, 0:others], zd_send.at[k], zd_recv.at[k])
        for v in range(4):
            forth(k, v, 0).start()

        @pl.when(k + 2 < SETS)
        def _():
            start_out(k + 2)

    def forth_own(k):
        for v in range(4):
            select(k, v, 0, zr[k, :, v * cols : (v + 1) * cols])

    def forth_1(k):
        forth_wait(k, 0)
        for v in range(4):
            select(k, v, 1, r1[k * 4 + v])
            forth(k, v, 1).start()

    def forth_2(k):
        forth_wait(k, 1)
        for v in range(4):
            forth(k, v, 2).start()

    def forth_3(k):
        forth_wait(k, 2)
        for v in range(4):
            forth(k, v, 3).start()

    def forth_near(k):
        for v in range(4):
            accumulate(k, v, 0, g3[k * 4 + v, 1:3, 0])

    def forth_far(k):
        forth_wait(k, 3)
        for v in range(4):
            accumulate(k, v, 1, f1[k * 4 + v])

    def back_3(k):
        for v in range(4):
            i = k * 4 + v
            result = dot(hid[...], w_down[:, columns(i, cols)]).astype(BF16)
            for r4 in (1, 0):
                for b in range(8):
                    r3, r2, r1_ = b >> 2, b >> 1 & 1, b & 1
                    inner = slice(r1_ * pad, (r1_ + 1) * pad)
                    c = block_of(v, r4, b)
                    if r4:
                        f1[i, r3, r2, inner, :] = result[c * pad : (c + 1) * pad]
                    else:
                        g3[i, 1 + r3, 0, r2, inner, :] = result[c * pad : (c + 1) * pad]
                if r4:
                    back(k, v, 3).start()

    def back_2(k):
        back_wait(k, 3)
        for v in range(4):
            back(k, v, 2).start()

    def back_1(k):
        back_wait(k, 2)
        for v in range(4):
            back(k, v, 1).start()

    def part_sum(k, v, r):
        i = k * 4 + v
        inner = slice(r * pad, (r + 1) * pad)
        near = g3[i, 0:2, :, 0, inner, :].reshape(4 * pad, cols)
        far = s2[i, :, :, inner, :].reshape(4 * pad, cols)
        return dot(weigh[v, r], jnp.concatenate([near, far], axis=0))

    def back_0(k):
        back_wait(k, 1)
        for v in range(4):
            r1[k * 4 + v] = part_sum(k, v, 1).astype(BF16)
            back(k, v, 0).start()

    def back_own(k):
        back_wait(k, 0)
        for v in range(4):
            own = part_sum(k, v, 0)
            zr[k, :, v * cols : (v + 1) * cols] = (own + p1[k * 4 + v].astype(F32)).astype(BF16)
        start_all(functools.partial(back_copy, k))
        zb[k, rows_of(g), :] = zr[k, rows_of(g), :]

    def back_out(k):
        settle(zb.at[k, 0:others], zc_send.at[k], zc_recv.at[k])
        out_ref[:, columns(k, set_cols)] = dot(give[...], zb[k]).astype(BF16)

    def staggered(stages, once):
        depth = 1 + max(lag for lag, _ in stages)

        def slot_step(t):
            for lag, stage in stages:
                k = t - lag

                @pl.when((k >= 0) & (k < SETS))
                def _(stage=stage, k=k):
                    stage(k)

            for at, extra in once:
                pl.when(t == at)(extra)

        loop(0, SETS + depth - 1, slot_step)

    def weights_here():
        for copy in weights:
            copy.wait()

    def weights_back():
        for v in range(4):
            for r in range(2):
                build_weigh(v, r)

    staggered(
        ((4, forth_far), (3, forth_3), (2, forth_2), (1, forth_1), (0, forth_0), (0, forth_own), (3, forth_near)),
        ((0, partners), (2, weights_here), (3, weights_back)),
    )
    for c in range(16):
        gated = acc[c, :, 0:width]
        upward = acc[c, :, width : 2 * width]
        hid[c * pad : (c + 1) * pad, :] = (gated / (1.0 + jnp.exp(-gated)) * upward).astype(BF16)
    staggered(((0, back_3), (1, back_2), (2, back_1), (3, back_0), (4, back_own), (6, back_out)), ())


def on_device(tokens, segment_ids, segment_count, gate_values, gate_weight, up_weight, down_weight):
    groups = lax.axis_size("group")
    model = tokens.shape[1]
    width = gate_weight.shape[2]
    held = groups * ROWS
    pad = groups * SLOTS
    cols = model // (4 * SETS)
    vmem = pl.BlockSpec(memory_space=pltpu.VMEM)
    hbm = pl.BlockSpec(memory_space=pl.ANY)
    dma = pltpu.SemaphoreType.DMA

    def per_set():
        return pltpu.VMEM((SETS, held, 4 * cols), BF16)

    def per_item(*shape):
        return pltpu.VMEM((SETS * 4,) + shape + (cols,), BF16)

    return pl.pallas_call(
        functools.partial(kernel, groups),
        out_shape=jax.ShapeDtypeStruct(tokens.shape, BF16),
        in_specs=[vmem, vmem, vmem, vmem, hbm, hbm, hbm],
        out_specs=vmem,
        scratch_shapes=[
            pltpu.VMEM((model, 2 * width), BF16),
            pltpu.VMEM((width, model), BF16),
            pltpu.VMEM((16, pad, 2 * width), F32),
            pltpu.VMEM((16 * pad, width), BF16),
            pltpu.VMEM((held, tokens.shape[0]), BF16),
            pltpu.VMEM((tokens.shape[0], held), BF16),
            pltpu.VMEM((held, 128), BF16),
            pltpu.VMEM((held, 128), BF16),
            pltpu.VMEM((4, held, 128), BF16),
            pltpu.VMEM((5, 32, held), F32),
            pltpu.VMEM((4, 2, 8 * pad, held), BF16),
            pltpu.VMEM((4, 2, held, 8 * pad), BF16),
            pltpu.VMEM((8 * pad, held), BF16),
            dma((3,)),
            dma, dma, dma((4,)), dma((4,)),
            *[dma((SETS,))] * 4,
            *[dma((4, SETS))] * 4,
            per_set(), per_set(), per_set(),
            per_item(held), per_item(held),
            per_item(3, 2, 2, 2 * pad),
            per_item(2, 2, 2 * pad), per_item(2, 2, 2 * pad),
        ],
        compiler_params=pltpu.CompilerParams(
            collective_id=0, has_side_effects=True, vmem_limit_bytes=56 * 1024 * 1024
        ),
    )(segment_ids.T, segment_count[None, :], gate_values.T, tokens, gate_weight, up_weight, down_weight)


def solution(mesh):
    return jax.shard_map(
        on_device,
        mesh=mesh,
        in_specs=(
            P(("group", "local"), None),
            P(("group", "local"), None),
            P(("group", "local")),
            P(("group", "local"), None),
            P(("group", "local"), None, None),
            P(("group", "local"), None, None),
            P(("group", "local"), None, None),
        ),
        out_specs=P(("group", "local"), None),
        check_vma=False,
    )
```
